32 devices in a mesh: dof: 16 (over z, x, core), snap: 2 (over y).
Axes of the slice: x: 2, y: 2, z: 4, core: 2. Of those that a mesh axis runs over, the one named last changes fastest.
Arguments:
- snapshots: float32 [65536, 1024], P('dof', 'snap'), may hold values from -19 to 19
Outputs:
- basis: float32 [65536, 1024], P('dof', 'snap')
- factor: float32 [1024, 1024], P(None, 'snap')
The draws below stay inside these ranges and needn't reach their ends.
All inputs are finite; a program needn't handle non-finite values.
Results may differ from the reference program's by a relative error of at most 0.00024.
Values sent between devices are 32-bit elements; how exact they have to be, the bound alone decides.
No kernel may reach another device: no remote copies, remote signals or barrier semaphores. Data moves between devices by JAX's collectives and lax.ppermute only.
A program may use at most 128 MiB of HBM per device.

```python
import math
import jax
import jax.numpy as jnp
from jax import lax

SNAPSHOT_COUNT = 1024
NDOF = 65536


def draw_snapshots(key, part):
    subkeys = jax.random.split(key, 4)
    position = jnp.arange(NDOF, dtype=jnp.float32)[:, None]
    sample_times = jnp.arange(SNAPSHOT_COUNT, dtype=jnp.float32)[None, :]
    angular_rate = jax.random.uniform(subkeys[0], (NDOF, 1), jnp.float32, 0.0, 0.5)
    phase_angles = jax.random.uniform(subkeys[1], (NDOF, 1), jnp.float32, -math.pi, math.pi)
    amplitude = jnp.exp(jax.random.uniform(subkeys[2], (NDOF, 1), jnp.float32, math.log(0.5), math.log(2.0)))
    amplitude = amplitude * (0.6 + 1.2 * position / NDOF)
    rotor_response = 1.2 * jnp.cos(angular_rate * sample_times + phase_angles)
    noises = jnp.clip(jax.random.normal(subkeys[3], (NDOF, SNAPSHOT_COUNT), jnp.float32), -4.0, 4.0)
    return amplitude * (rotor_response + noises)


def setup_inputs(seed: int = 0) -> dict:
    streams_of = jax.random.split(jax.random.key(seed), 2)
    snapshots = draw_snapshots(jax.random.fold_in(streams_of[1], 71), 0)
    return {"snapshots": snapshots}


def reference(snapshots):
    gram = jnp.dot(snapshots.T.astype(jnp.float32), snapshots.astype(jnp.float32), preferred_element_type=jnp.float32, precision=lax.Precision.HIGHEST)
    lower = jnp.linalg.cholesky(gram)
    identity = jnp.eye(SNAPSHOT_COUNT, dtype=jnp.float32)
    inverse = jax.scipy.linalg.solve_triangular(lower, identity, lower=True).T
    root_rows = jnp.sqrt(jnp.float32(NDOF))
    basis = jnp.dot(snapshots.astype(jnp.float32), inverse.astype(jnp.float32), preferred_element_type=jnp.float32, precision=lax.Precision.HIGHEST) * root_rows
    factor = lower.T / root_rows
    return (basis, factor)
```

```python
import functools

import jax
import jax.numpy as jnp
from jax import lax
from jax.experimental import pallas as pl
from jax.experimental.pallas import tpu as pltpu
from jax.sharding import PartitionSpec as P

F32 = jnp.float32
BF16 = jnp.bfloat16
HIGHEST = lax.Precision.HIGHEST
VMEM = pltpu.VMEM
BLOCK = 128
GROUP = 8
TILE = 512


def params(megabytes):
    return pltpu.CompilerParams(vmem_limit_bytes=megabytes * 1024 * 1024)


def whole(count):
    return [pl.BlockSpec(memory_space=VMEM)] * count


def dot(a, b, contract, precision=None):
    return lax.dot_general(
        a, b, ((contract[:1], contract[1:]), ((), ())), precision=precision, preferred_element_type=F32
    )


def split(x):
    high = x.astype(BF16)
    return high, (x - high.astype(F32)).astype(BF16)


def dot3(a, b, contract):
    ah, al = split(a)
    bh, bl = split(b)
    return dot(ah, bh, contract) + (dot(ah, bl, contract) + dot(al, bh, contract))


def own_gram_kernel(scale, s_ref, g_ref, high_acc, mixed_acc):
    step = pl.program_id(0)

    @pl.when(step == 0)
    def _():
        high_acc[...] = jnp.zeros_like(high_acc)
        mixed_acc[...] = jnp.zeros_like(mixed_acc)

    high, low = split(s_ref[...])
    high_acc[...] += dot(high, high, (0, 0)) + dot(low, low, (0, 0))
    mixed_acc[...] += dot(high, low, (0, 0))

    @pl.when(step == pl.num_programs(0) - 1)
    def _():
        mixed = mixed_acc[...]
        g_ref[...] = (high_acc[...] + (mixed + mixed.T)) * scale


def own_gram(s, scale):
    rows, width = s.shape
    square = (width, width)
    return pl.pallas_call(
        functools.partial(own_gram_kernel, scale),
        grid=(rows // TILE,),
        out_shape=jax.ShapeDtypeStruct(square, F32),
        in_specs=[pl.BlockSpec((TILE, width), lambda i: (i, 0))],
        out_specs=pl.BlockSpec(square, lambda i: (0, 0)),
        scratch_shapes=[pltpu.VMEM(square, F32), pltpu.VMEM(square, F32)],
        compiler_params=params(40),
        cost_estimate=pl.CostEstimate(
            flops=6 * rows * width * width, bytes_accessed=4 * rows * width, transcendentals=0
        ),
        name="own_gram",
    )(s)


def cross_gram_kernel(scale, side_ref, own_ref, other_ref, before_ref, g_ref):
    step = pl.program_id(0)

    @pl.when(step == 0)
    def _():
        g_ref[...] = before_ref[...]

    first = side_ref[0] == 0
    own, other = own_ref[...], other_ref[...]
    left = jnp.where(first, own, other)
    right = jnp.where(first, other, own)
    lh, ll = split(left)
    rh, rl = split(right * scale)
    g_ref[...] += (dot(lh, rh, (0, 0)) + dot(ll, rl, (0, 0))) + (dot(lh, rl, (0, 0)) + dot(ll, rh, (0, 0)))


def cross_gram(side, own, other, before, offset, scale):
    width = own.shape[1]
    rows = other.shape[0]
    square = (width, width)
    tile = min(TILE, rows)
    half = own.shape[0] // 2 // tile
    start = offset // tile
    return pl.pallas_call(
        functools.partial(cross_gram_kernel, scale),
        grid_spec=pltpu.PrefetchScalarGridSpec(
            num_scalar_prefetch=1,
            grid=(rows // tile,),
            in_specs=[
                pl.BlockSpec((tile, width), lambda i, side: (i + start + (1 - side[0]) * half, 0)),
                pl.BlockSpec((tile, width), lambda i, side: (i, 0)),
                pl.BlockSpec(square, lambda i, side: (0, 0)),
            ],
            out_specs=pl.BlockSpec(square, lambda i, side: (0, 0)),
        ),
        out_shape=jax.ShapeDtypeStruct(square, F32),
        compiler_params=params(40),
        cost_estimate=pl.CostEstimate(
            flops=8 * rows * width * width, bytes_accessed=8 * rows * width, transcendentals=0
        ),
        name="cross_gram",
    )(side, own, other, before)


def factor_block(a, x):
    count, width = len(a), a[0].shape[1]
    shape = (GROUP, width)
    row = lax.broadcasted_iota(jnp.int32, shape, 0)
    lane = lax.broadcasted_iota(jnp.int32, shape, 1)
    upper, inverse = [], []
    for p in range(count):
        c = GROUP * p
        pa = [jnp.broadcast_to(a[p][k : k + 1, :], shape) for k in range(GROUP)]
        px = [jnp.broadcast_to(x[p][k : k + 1, :], shape) for k in range(GROUP)]
        s = [
            [jnp.broadcast_to(pa[k][:, c + l : c + l + 1], shape) if l >= k else None for l in range(GROUP)]
            for k in range(GROUP)
        ]
        reciprocal = []
        for k in range(GROUP):
            reciprocal.append(1.0 / s[k][k])
            for l in range(k + 1, GROUP):
                m = s[k][l] * reciprocal[k]
                for t in range(l, GROUP):
                    s[l][t] = s[l][t] - m * s[k][t]
                pa[l] = pa[l] - m * pa[k]
                px[l] = px[l] - m * px[k]
        for r in range(p + 1, count):
            columns = [jnp.broadcast_to(a[r][:, c + l : c + l + 1], shape) for l in range(GROUP)]
            for k in range(GROUP):
                m = columns[k] * reciprocal[k]
                for t in range(k + 1, GROUP):
                    columns[t] = columns[t] - m * s[k][t]
                a[r] = a[r] - m * pa[k]
                x[r] = x[r] - m * px[k]
        ua, ux = None, None
        for k in range(GROUP):
            root = lax.rsqrt(s[k][k])
            va, vx = pa[k] * root, px[k] * root
            ua = va if k == 0 else jnp.where(row == k, va, ua)
            ux = vx if k == 0 else jnp.where(row == k, vx, ux)
        upper.append(jnp.where(lane >= row + c, ua, 0.0))
        inverse.append(ux)
    return upper, inverse


def factor_whole(a_ref, r_ref, x_ref, e_ref):
    order = a_ref.shape[0]
    blocks = order // BLOCK
    groups = BLOCK // GROUP
    r_ref[...] = jnp.zeros_like(r_ref)
    x_ref[...] = jnp.zeros_like(x_ref)
    row = lax.broadcasted_iota(jnp.int32, (GROUP, BLOCK), 0)
    lane = lax.broadcasted_iota(jnp.int32, (GROUP, BLOCK), 1)

    def body(b, carry):
        start = pl.multiple_of(b * BLOCK, BLOCK)
        here = pl.ds(start, BLOCK)
        a = [a_ref[pl.ds(start + GROUP * i, GROUP), here] for i in range(groups)]
        x = [jnp.where(lane == row + GROUP * i, 1.0, 0.0) for i in range(groups)]
        upper, inverse = factor_block(a, x)
        for i in range(groups):
            r_ref[pl.ds(start + GROUP * i, GROUP), here] = upper[i]
            e_ref[pl.ds(GROUP * i, GROUP), :] = inverse[i]
        for k in range(blocks):

            @pl.when(b == k)
            def _():
                lo, hi = k * BLOCK, (k + 1) * BLOCK
                e = e_ref[...]
                x_ref[lo:hi, lo:hi] = e
                if k > 0:
                    x_ref[lo:hi, :lo] = dot(e, x_ref[lo:hi, :lo], (1, 0), HIGHEST)
                if hi < order:
                    strip = dot(e, a_ref[lo:hi, hi:], (1, 0), HIGHEST)
                    r_ref[lo:hi, hi:] = strip
                    a_ref[hi:, hi:] -= dot(strip, strip, (0, 0), HIGHEST)
                    x_ref[hi:, :hi] -= dot(strip, x_ref[lo:hi, :hi], (0, 0), HIGHEST)

        return carry

    lax.fori_loop(0, blocks, body, 0)


def first_factor_kernel(g_ref, r_ref, x_ref, a_ref, e_ref):
    a_ref[...] = g_ref[...]
    factor_whole(a_ref, r_ref, x_ref, e_ref)


def first_factor(gram):
    order = gram.shape[0]
    square = jax.ShapeDtypeStruct((order, order), F32)
    return pl.pallas_call(
        first_factor_kernel,
        out_shape=[square, square],
        in_specs=whole(1),
        out_specs=whole(2),
        scratch_shapes=[pltpu.VMEM((order, order), F32), pltpu.VMEM((BLOCK, BLOCK), F32)],
        compiler_params=params(40),
        cost_estimate=pl.CostEstimate(flops=30 * order**3, bytes_accessed=12 * order * order, transcendentals=0),
        name="first_factor",
    )(gram)


def second_factor_kernel(cross_ref, gram_ref, x0_ref, r01_ref, r_ref, x_ref, w01_ref, a_ref, e_ref):
    x0 = x0_ref[...]
    r01 = dot(x0, cross_ref[...], (1, 0), HIGHEST)
    r01_ref[...] = r01
    a_ref[...] = gram_ref[...] - dot(r01, r01, (0, 0), HIGHEST)
    factor_whole(a_ref, r_ref, x_ref, e_ref)
    u = dot(x0, r01_ref[...], (0, 0), HIGHEST)
    w01_ref[...] = -dot(u, x_ref[...], (1, 1), HIGHEST)


def second_factor(cross, gram, x0):
    order = gram.shape[0]
    square = jax.ShapeDtypeStruct((order, order), F32)
    return pl.pallas_call(
        second_factor_kernel,
        out_shape=[square] * 4,
        in_specs=whole(3),
        out_specs=whole(4),
        scratch_shapes=[pltpu.VMEM((order, order), F32), pltpu.VMEM((BLOCK, BLOCK), F32)],
        compiler_params=params(40),
        cost_estimate=pl.CostEstimate(flops=60 * order**3, bytes_accessed=28 * order * order, transcendentals=0),
        name="second_factor",
    )(cross, gram, x0)


def basis_kernel(counts, side_ref, own_ref, *refs):
    chunks = refs[: len(counts)]
    x0_ref, x1_ref, w01_ref, out_ref, oh, ol, ch, cl = refs[len(counts) :]
    step = pl.program_id(0)

    @pl.when(step == 0)
    def _():
        first = side_ref[0] == 0
        own = jnp.where(first, x0_ref[...], x1_ref[...]).T
        oh[...], ol[...] = split(own)
        cross = jnp.where(first, 0.0, w01_ref[...])
        ch[...], cl[...] = split(cross)

    def product(x, high, low):
        xh, xl = split(x)
        return dot(xh, high[...], (1, 0)) + (dot(xh, low[...], (1, 0)) + dot(xl, high[...], (1, 0)))

    start = 0
    for chunk, count in zip(chunks, counts):

        @pl.when((step >= start) & (step < start + count))
        def _():
            out_ref[...] = product(own_ref[...], oh, ol) + product(chunk[...], ch, cl)

        start += count


def whitened(side, own, chunks, x0, x1, w01):
    rows, width = own.shape
    counts = tuple(c.shape[0] // TILE for c in chunks)
    starts = [sum(counts[:i]) for i in range(len(counts))]
    square = (width, width)

    def chunk_spec(start, count):
        return pl.BlockSpec((TILE, width), lambda i, side: (jnp.clip(i - start, 0, count - 1), 0))

    fixed = pl.BlockSpec(square, lambda i, side: (0, 0))
    return pl.pallas_call(
        functools.partial(basis_kernel, counts),
        grid_spec=pltpu.PrefetchScalarGridSpec(
            num_scalar_prefetch=1,
            grid=(rows // TILE,),
            in_specs=[pl.BlockSpec((TILE, width), lambda i, side: (i, 0))]
            + [chunk_spec(s, c) for s, c in zip(starts, counts)]
            + [fixed] * 3,
            out_specs=pl.BlockSpec((TILE, width), lambda i, side: (i, 0)),
            scratch_shapes=[pltpu.VMEM(square, BF16)] * 4,
        ),
        out_shape=jax.ShapeDtypeStruct((rows, width), F32),
        compiler_params=params(48),
        cost_estimate=pl.CostEstimate(
            flops=12 * rows * width * width, bytes_accessed=12 * rows * width, transcendentals=0
        ),
        name="whitened",
    )(side, own, *chunks, x0, x1, w01)


def flip(x, bit):
    count = lax.axis_size("dof")
    return lax.ppermute(x, "dof", [(i, i ^ bit) for i in range(count)])


def flip_side(x, bit):
    count = lax.axis_size("dof") * 2
    return lax.ppermute(x, ("dof", "snap"), [(i, i ^ (2 * bit + 1)) for i in range(count)])


def halve(x, upper, send):
    half = x.shape[0] // 2
    low, high = x[:half], x[half:]
    return jnp.where(upper, high, low) + send(jnp.where(upper, low, high))


def double(x, upper, send):
    other = send(x)
    return jnp.concatenate([jnp.where(upper, other, x), jnp.where(upper, x, other)])


def on_device(snapshots):
    rows, width = snapshots.shape
    count = lax.axis_size("dof")
    scale = 1.0 / (rows * count)
    me, side = lax.axis_index("dof"), lax.axis_index("snap")
    side_operand = jnp.full((1,), side, jnp.int32)
    across = 2
    outer = [1] + [1 << i for i in range(2, count.bit_length() - 1)]

    def bit(k):
        return (me & k) != 0

    half = rows // 2
    quarter = half // 2
    swap = [(0, 1), (1, 0)]
    sent = [lax.dynamic_slice_in_dim(snapshots, side * half + j * quarter, quarter, 0) for j in range(2)]
    arrived = [lax.ppermute(x, "snap", swap) for x in sent]
    rest = lax.ppermute(snapshots[half:], "snap", [(0, 1)])

    own = own_gram(snapshots, scale)
    second = lax.psum(own, "dof")
    shard = own
    for k in outer + [across]:
        shard = halve(shard, bit(k), functools.partial(flip, bit=k))
    received = flip_side(shard, across)
    shard = jnp.where(side == 0, shard, received)
    shard = double(shard, bit(across) ^ (side == 1), functools.partial(flip, bit=across))
    for k in outer[::-1]:
        shard = double(shard, bit(k), functools.partial(flip, bit=k))
    r00, x00 = first_factor(shard)

    cross = jnp.zeros((width, width), F32)
    for j in range(2):
        cross = cross_gram(side_operand, snapshots, arrived[j], cross, j * quarter, scale)
    for k in outer:
        cross = halve(cross, bit(k), functools.partial(flip, bit=k))
    cross = halve(cross, side == 1, functools.partial(flip_side, bit=across))
    cross = cross + flip(cross, across)
    cross = double(cross, side == 1, functools.partial(flip_side, bit=across))
    for k in outer[::-1]:
        cross = double(cross, bit(k), functools.partial(flip, bit=k))

    r01, r11, x11, w01 = second_factor(cross, second, x00)
    basis = whitened(side_operand, snapshots, arrived + [rest], x00, x11, w01)
    factor = jnp.concatenate([jnp.where(side == 0, r00, r01), jnp.where(side == 0, 0.0, r11)])
    return (basis, factor)


def solution(mesh):
    in_specs = (P("dof", "snap"),)
    out_specs = (P("dof", "snap"), P(None, "snap"))
    return jax.shard_map(
        on_device, mesh=mesh, in_specs=in_specs, out_specs=out_specs, check_vma=False
    )
```

```python
import functools
import math

import jax
import jax.numpy as jnp
from jax import lax
from jax.experimental import pallas as pl
from jax.experimental.pallas import tpu as pltpu
from jax.sharding import PartitionSpec as P

F32 = jnp.float32
BF16 = jnp.bfloat16
HIGHEST = lax.Precision.HIGHEST
VMEM = pltpu.VMEM
BLOCK = 128
GROUP = 8
TILE = 512
COST = pl.CostEstimate(flops=1, bytes_accessed=1, transcendentals=0)


def params(megabytes):
    return pltpu.CompilerParams(vmem_limit_bytes=megabytes * 1024 * 1024)


def whole(count):
    return [pl.BlockSpec(memory_space=VMEM)] * count


def dot(a, b, contract, precision=None):
    return lax.dot_general(
        a, b, ((contract[:1], contract[1:]), ((), ())), precision=precision, preferred_element_type=F32
    )


def split(x):
    high = x.astype(BF16)
    return high, (x - high.astype(F32)).astype(BF16)


def dot3(a, b, contract):
    ah, al = split(a)
    bh, bl = split(b)
    return dot(ah, bh, contract) + (dot(ah, bl, contract) + dot(al, bh, contract))


def block_pairs(blocks):
    return [(i, j) for i in range(blocks) for j in range(i, blocks)]


def own_gram_kernel(scale, spans, side_ref, s_ref, g_ref, *refs):
    copies, (high_acc, mixed_acc) = refs[:-2], refs[-2:]
    step = pl.program_id(0)
    half = high_acc.shape[0] // 2

    @pl.when(step == 0)
    def _():
        high_acc[...] = jnp.zeros_like(high_acc)
        mixed_acc[...] = jnp.zeros_like(mixed_acc)

    block = s_ref[...]
    for copy, (start, shift, count) in zip(copies, spans):
        begin = start + shift * side_ref[0]

        @pl.when((step >= begin) & (step < begin + count))
        def _():
            copy[...] = block

    high, low = split(block)
    high_acc[:half] += dot(high[:, :half], high, (0, 0)) + dot(low[:, :half], low, (0, 0))
    high_acc[half:, half:] += dot(high[:, half:], high[:, half:], (0, 0)) + dot(low[:, half:], low[:, half:], (0, 0))
    mixed_acc[...] += dot(high, low, (0, 0))

    @pl.when(step == pl.num_programs(0) - 1)
    def _():
        for k, (i, j) in enumerate(block_pairs(high_acc.shape[0] // BLOCK)):
            rows, columns = pl.ds(i * BLOCK, BLOCK), pl.ds(j * BLOCK, BLOCK)
            mixed = mixed_acc[rows, columns] + mixed_acc[columns, rows].T
            g_ref[pl.ds(k * BLOCK, BLOCK), :] = (high_acc[rows, columns] + mixed) * scale


def own_gram(side, s, scale, spans):
    rows, width = s.shape
    square = (width, width)
    packed = (len(block_pairs(width // BLOCK)) * BLOCK, BLOCK)

    def copy_spec(start, shift, count):
        return pl.BlockSpec((TILE, width), lambda i, side: (jnp.clip(i - start - shift * side[0], 0, count - 1), 0))

    return pl.pallas_call(
        functools.partial(own_gram_kernel, scale, spans),
        grid_spec=pltpu.PrefetchScalarGridSpec(
            num_scalar_prefetch=1,
            grid=(rows // TILE,),
            in_specs=[pl.BlockSpec((TILE, width), lambda i, side: (i, 0))],
            out_specs=[pl.BlockSpec(packed, lambda i, side: (0, 0))] + [copy_spec(*span) for span in spans],
            scratch_shapes=[pltpu.VMEM(square, F32), pltpu.VMEM(square, F32)],
        ),
        out_shape=[jax.ShapeDtypeStruct(packed, F32)]
        + [jax.ShapeDtypeStruct((count * TILE, width), F32) for _, _, count in spans],
        compiler_params=params(60),
        cost_estimate=COST,
        name="own_gram",
    )(side, s)


def cross_gram_kernel(scale, resume, counts, side_ref, own_ref, *refs):
    chunks, before_ref, g_ref = refs[: len(counts)], refs[len(counts)], refs[-1]
    step = pl.program_id(0)
    first = side_ref[0] == 0

    @pl.when(step == 0)
    def _():
        g_ref[...] = before_ref[...] if resume else jnp.zeros_like(g_ref)

    begin = 0
    for chunk, count in zip(chunks, counts):

        @pl.when((step >= begin) & (step < begin + count))
        def _():
            own, other = own_ref[...], chunk[...]
            left = jnp.where(first, own, other)
            right = jnp.where(first, other, own)
            lh, ll = split(left)
            rh, rl = split(right * scale)
            g_ref[...] += (dot(lh, rh, (0, 0)) + dot(ll, rl, (0, 0))) + (dot(lh, rl, (0, 0)) + dot(ll, rh, (0, 0)))

        begin += count


def cross_gram(side, own, chunks, before, after, offset, scale):
    rows, width = own.shape
    counts = tuple(c.shape[0] // TILE for c in chunks)
    starts = [sum(counts[:i]) for i in range(len(counts))]
    square = (width, width)
    half = rows // 2 // TILE
    start = offset // TILE

    def chunk_spec(begin, count):
        return pl.BlockSpec((TILE, width), lambda i, side: (jnp.clip(i - begin, 0, count - 1), 0))

    in_specs = [pl.BlockSpec((TILE, width), lambda i, side: (i + start + (1 - side[0]) * half, 0))]
    in_specs += [chunk_spec(b, c) for b, c in zip(starts, counts)]
    in_specs += [pl.BlockSpec(square, lambda i, side: (0, 0))] * (before is not None)
    in_specs += [pl.BlockSpec(memory_space=pl.ANY)] * len(after)
    return pl.pallas_call(
        functools.partial(cross_gram_kernel, scale, before is not None, counts),
        grid_spec=pltpu.PrefetchScalarGridSpec(
            num_scalar_prefetch=1,
            grid=(sum(counts),),
            in_specs=in_specs,
            out_specs=pl.BlockSpec(square, lambda i, side: (0, 0)),
        ),
        out_shape=jax.ShapeDtypeStruct(square, F32),
        compiler_params=params(60),
        cost_estimate=COST,
        name="cross_gram",
    )(side, own, *chunks, *([] if before is None else [before]), *after)


def factor_block(a, x):
    count, width = len(a), a[0].shape[1]
    shape = (GROUP, width)
    row = lax.broadcasted_iota(jnp.int32, shape, 0)
    lane = lax.broadcasted_iota(jnp.int32, shape, 1)
    upper, inverse = [], []
    for p in range(count):
        c = GROUP * p
        pa = [jnp.broadcast_to(a[p][k : k + 1, :], shape) for k in range(GROUP)]
        px = [jnp.broadcast_to(x[p][k : k + 1, :], shape) for k in range(GROUP)]
        s = [
            [jnp.broadcast_to(pa[k][:, c + l : c + l + 1], shape) if l >= k else None for l in range(GROUP)]
            for k in range(GROUP)
        ]
        reciprocal = []
        for k in range(GROUP):
            reciprocal.append(1.0 / s[k][k])
            for l in range(k + 1, GROUP):
                m = s[k][l] * reciprocal[k]
                for t in range(l, GROUP):
                    s[l][t] = s[l][t] - m * s[k][t]
                pa[l] = pa[l] - m * pa[k]
                px[l] = px[l] - m * px[k]
        for r in range(p + 1, count):
            columns = [jnp.broadcast_to(a[r][:, c + l : c + l + 1], shape) for l in range(GROUP)]
            for k in range(GROUP):
                m = columns[k] * reciprocal[k]
                for t in range(k + 1, GROUP):
                    columns[t] = columns[t] - m * s[k][t]
                a[r] = a[r] - m * pa[k]
                x[r] = x[r] - m * px[k]
        ua, ux = None, None
        for k in range(GROUP):
            root = lax.rsqrt(s[k][k])
            va, vx = pa[k] * root, px[k] * root
            ua = va if k == 0 else jnp.where(row == k, va, ua)
            ux = vx if k == 0 else jnp.where(row == k, vx, ux)
        upper.append(jnp.where(lane >= row + c, ua, 0.0))
        inverse.append(ux)
    return upper, inverse


def factor_whole(a_ref, r_ref, x_ref, e_ref):
    order = a_ref.shape[0]
    blocks = order // BLOCK
    groups = BLOCK // GROUP
    r_ref[...] = jnp.zeros_like(r_ref)
    x_ref[...] = jnp.zeros_like(x_ref)
    row = lax.broadcasted_iota(jnp.int32, (GROUP, BLOCK), 0)
    lane = lax.broadcasted_iota(jnp.int32, (GROUP, BLOCK), 1)

    def body(b, carry):
        start = pl.multiple_of(b * BLOCK, BLOCK)
        here = pl.ds(start, BLOCK)
        a = [a_ref[pl.ds(start + GROUP * i, GROUP), here] for i in range(groups)]
        x = [jnp.where(lane == row + GROUP * i, 1.0, 0.0) for i in range(groups)]
        upper, inverse = factor_block(a, x)
        for i in range(groups):
            r_ref[pl.ds(start + GROUP * i, GROUP), here] = upper[i]
            e_ref[pl.ds(GROUP * i, GROUP), :] = inverse[i]
        for k in range(blocks):

            @pl.when(b == k)
            def _():
                lo, hi = k * BLOCK, (k + 1) * BLOCK
                e = e_ref[...]
                x_ref[lo:hi, lo:hi] = e
                if k > 0:
                    x_ref[lo:hi, :lo] = dot(e, x_ref[lo:hi, :lo], (1, 0), HIGHEST)
                if hi < order:
                    strip = dot(e, a_ref[lo:hi, hi:], (1, 0), HIGHEST)
                    r_ref[lo:hi, hi:] = strip
                    a_ref[hi:, hi:] -= dot(strip, strip, (0, 0), HIGHEST)
                    x_ref[hi:, :hi] -= dot(strip, x_ref[lo:hi, :hi], (0, 0), HIGHEST)

        return carry

    lax.fori_loop(0, blocks, body, 0)


def unpack(packed_ref, a_ref):
    for k, (i, j) in enumerate(block_pairs(a_ref.shape[0] // BLOCK)):
        a_ref[pl.ds(i * BLOCK, BLOCK), pl.ds(j * BLOCK, BLOCK)] = packed_ref[pl.ds(k * BLOCK, BLOCK), :]


def first_factor_kernel(g_ref, r_ref, x_ref, a_ref, e_ref):
    unpack(g_ref, a_ref)
    factor_whole(a_ref, r_ref, x_ref, e_ref)


def first_factor(packed, order):
    square = jax.ShapeDtypeStruct((order, order), F32)
    return pl.pallas_call(
        first_factor_kernel,
        out_shape=[square, square],
        in_specs=whole(1),
        out_specs=whole(2),
        scratch_shapes=[pltpu.VMEM((order, order), F32), pltpu.VMEM((BLOCK, BLOCK), F32)],
        compiler_params=params(40),
        cost_estimate=COST,
        name="first_factor",
    )(packed)


def second_factor_kernel(side_ref, cross_ref, g_ref, r00_ref, x0_ref, f_ref, *refs):
    own_high, own_low, other_high, other_low, a_ref, r_ref, x_ref, e_ref = refs
    order = a_ref.shape[0]
    first = side_ref[0] == 0
    x0 = x0_ref[...]
    r01 = dot(x0, cross_ref[...], (1, 0), HIGHEST)
    unpack(g_ref, a_ref)
    a_ref[...] -= dot(r01, r01, (0, 0), HIGHEST)
    u = dot3(x0, r01, (0, 0))
    f_ref[:order] = jnp.where(first, r00_ref[...], r01)
    factor_whole(a_ref, r_ref, x_ref, e_ref)
    f_ref[order:] = jnp.where(first, 0.0, r_ref[...])
    x1 = x_ref[...]
    own_high[...], own_low[...] = split(jnp.where(first, x0, x1).T)
    other_high[...], other_low[...] = split(jnp.where(first, 0.0, -dot3(u, x1, (1, 1))))


def second_factor(side, cross, packed, r00, x0):
    order = cross.shape[0]
    square = (order, order)
    return pl.pallas_call(
        second_factor_kernel,
        out_shape=[jax.ShapeDtypeStruct((2 * order, order), F32)] + [jax.ShapeDtypeStruct(square, BF16)] * 4,
        in_specs=[pl.BlockSpec(memory_space=pltpu.SMEM)] + whole(4),
        out_specs=whole(5),
        scratch_shapes=[pltpu.VMEM(square, F32)] * 3 + [pltpu.VMEM((BLOCK, BLOCK), F32)],
        compiler_params=params(40),
        cost_estimate=COST,
        name="second_factor",
    )(side, cross, packed, r00, x0)


def basis_kernel(counts, own_ref, *refs):
    chunks = refs[: len(counts)]
    own_high, own_low, other_high, other_low = refs[len(counts) : len(counts) + 4]
    out_ref = refs[-1]
    step = pl.program_id(0)

    def product(x, high, low):
        xh, xl = split(x)
        return dot(xh, high[...], (1, 0)) + (dot(xh, low[...], (1, 0)) + dot(xl, high[...], (1, 0)))

    begin = 0
    for chunk, count in zip(chunks, counts):

        @pl.when((step >= begin) & (step < begin + count))
        def _():
            out_ref[...] = product(own_ref[...], own_high, own_low) + product(chunk[...], other_high, other_low)

        begin += count


def whitened(own, chunks, factors, row, before):
    rows, width = own.shape
    counts = tuple(c.shape[0] // TILE for c in chunks)
    starts = [sum(counts[:i]) for i in range(len(counts))]
    offset = row // TILE

    def chunk_spec(begin, count):
        return pl.BlockSpec((TILE, width), lambda i: (jnp.clip(i - begin, 0, count - 1), 0))

    in_specs = [pl.BlockSpec((TILE, width), lambda i: (i + offset, 0))]
    in_specs += [chunk_spec(b, c) for b, c in zip(starts, counts)]
    in_specs += [pl.BlockSpec((width, width), lambda i: (0, 0))] * 4
    operands = [own, *chunks, *factors]
    aliases = {}
    if before is not None:
        aliases = {len(operands): 0}
        in_specs.append(pl.BlockSpec(memory_space=pl.ANY))
        operands.append(before)
    return pl.pallas_call(
        functools.partial(basis_kernel, counts),
        grid=(sum(counts),),
        in_specs=in_specs,
        out_specs=pl.BlockSpec((TILE, width), lambda i: (i + offset, 0)),
        out_shape=jax.ShapeDtypeStruct((rows, width), F32),
        input_output_aliases=aliases,
        compiler_params=params(60),
        cost_estimate=COST,
        name="whitened",
    )(*operands)


def flip(x, order, step):
    count = lax.axis_size("dof")
    return lax.ppermute(x, "dof", [(i, i ^ order[i % 2][step]) for i in range(count)])


def flip_side(x, order):
    count = lax.axis_size("dof")
    pairs = [(2 * i + j, 2 * (i ^ order[i % 2][-1]) + 1 - j) for i in range(count) for j in range(2)]
    return lax.ppermute(x, ("dof", "snap"), pairs)


def halve(x, upper, send):
    half = x.shape[0] // 2
    low, high = x[:half], x[half:]
    return jnp.where(upper, high, low) + send(jnp.where(upper, low, high))


def double_with(x, other, upper, axis=0):
    return jnp.concatenate([jnp.where(upper, other, x), jnp.where(upper, x, other)], axis)


def double(x, upper, send, axis=0):
    return double_with(x, send(x), upper, axis)


def on_device(snapshots):
    rows, width = snapshots.shape
    count = lax.axis_size("dof")
    scale = 1.0 / (rows * count)
    me, side = lax.axis_index("dof"), lax.axis_index("snap")
    side_operand = jnp.full((1,), side, jnp.int32)
    bits = [1 << i for i in range(1, count.bit_length() - 1)]
    order = ([1] + bits[1:] + bits[:1], [1] + bits)
    steps = list(range(len(order[0])))

    def bit(step):
        return (me & jnp.where(me % 2 == 0, order[0][step], order[1][step])) != 0

    def send(step):
        return lambda x: flip(x, order, step)

    def send_side(x):
        return flip_side(x, order)

    def reduce_own(i, carry):
        shard = carry[0]
        for k in steps:
            shard = halve(shard, bit(k), send(k))
        received = send_side(shard)
        upper = bit(steps[-1]) ^ (side == 1)
        first = jnp.where(side == 0, shard, received)
        second = jnp.where(side == 0, received, shard)
        first = double(first, upper, send(steps[-1]))
        second = double(second, ~upper, send(steps[-1]))
        for k in steps[-2::-1]:
            first = double(first, bit(k), send(k))
            second = double(second, bit(k), send(k))
        return first, second

    def reduce_cross(i, cross):
        for k in steps[:-1]:
            cross = halve(cross, bit(k), send(k))
        cross = halve(cross, side == 1, send_side)
        cross = cross + send(steps[-1])(cross)
        cross = double(cross, side == 1, send_side)
        for k in steps[-2::-1]:
            cross = double(cross, bit(k), send(k))
        return cross

    half = rows // 2 // TILE
    parts = [half // 4, half // 2, half - half // 4 - half // 2]
    rests = [3 * half // 4, half - 3 * half // 4]
    spans = [(parts[0], half, parts[1]), (parts[0] + parts[1], half, parts[2])]
    spans += [(half, 0, rests[0]), (half + rests[0], 0, rests[1])]

    def swap(x):
        return lax.ppermute(x, "snap", [(0, 1), (1, 0)])

    def one_way(x):
        return lax.ppermute(x, "snap", [(0, 1)])

    def late(x, after):
        return lax.optimization_barrier((x, after))[0]

    once = 1 + jnp.minimum(side, 0)
    arrived = [swap(lax.dynamic_slice_in_dim(snapshots, side * half * TILE, parts[0] * TILE, 0))]
    own, send1, send2, send3, send4 = own_gram(side_operand, snapshots, scale, spans)
    arrived.append(swap(send1))
    first, second = lax.fori_loop(0, once, reduce_own, (own, own))
    arrived.append(swap(late(send2, first)))
    r00, x00 = first_factor(first, width)
    arrived.append(one_way(late(send3, r00)))
    early = parts[0] + parts[1]
    cross = cross_gram(side_operand, snapshots, arrived[:2], None, [x00, second], 0, scale)
    arrived.append(one_way(late(send4, cross)))
    cross = cross_gram(side_operand, snapshots, arrived[2:3], cross, [], early * TILE, scale)
    cross = lax.fori_loop(0, once, reduce_cross, cross)
    factor, *factors = second_factor(side_operand, cross, second, r00, x00)
    basis = whitened(snapshots, arrived[:-1], factors, 0, None)
    basis = whitened(snapshots, arrived[-1:], factors, (half + rests[0]) * TILE, basis)
    return (basis, factor)


def solution(mesh):
    in_specs = (P("dof", "snap"),)
    out_specs = (P("dof", "snap"), P(None, "snap"))
    return jax.shard_map(
        on_device, mesh=mesh, in_specs=in_specs, out_specs=out_specs, check_vma=False
    )
```

```python
import functools
import math

import jax
import jax.numpy as jnp
from jax import lax
from jax.experimental import pallas as pl
from jax.experimental.pallas import tpu as pltpu
from jax.sharding import PartitionSpec as P

F32 = jnp.float32
BF16 = jnp.bfloat16
HIGHEST = lax.Precision.HIGHEST
VMEM = pltpu.VMEM
BLOCK = 128
GROUP = 8
TILE = 512
COST = pl.CostEstimate(flops=1, bytes_accessed=1, transcendentals=0)


def params(megabytes):
    return pltpu.CompilerParams(vmem_limit_bytes=megabytes * 1024 * 1024)


def whole(count):
    return [pl.BlockSpec(memory_space=VMEM)] * count


def dot(a, b, contract, precision=None):
    return lax.dot_general(
        a, b, ((contract[:1], contract[1:]), ((), ())), precision=precision, preferred_element_type=F32
    )


def split(x):
    high = x.astype(BF16)
    return high, (x - high.astype(F32)).astype(BF16)


def dot3(a, b, contract):
    ah, al = split(a)
    bh, bl = split(b)
    return dot(ah, bh, contract) + (dot(ah, bl, contract) + dot(al, bh, contract))


def block_pairs(blocks):
    return [(i, j) for i in range(blocks) for j in range(i, blocks)]


def own_gram_kernel(scale, spans, side_ref, s_ref, g_ref, *refs):
    copies, (high_acc, mixed_acc) = refs[:-2], refs[-2:]
    step = pl.program_id(0)
    half = high_acc.shape[0] // 2

    @pl.when(step == 0)
    def _():
        high_acc[...] = jnp.zeros_like(high_acc)
        mixed_acc[...] = jnp.zeros_like(mixed_acc)

    block = s_ref[...]
    for copy, (start, shift, count) in zip(copies, spans):
        begin = start + shift * side_ref[0]

        @pl.when((step >= begin) & (step < begin + count))
        def _():
            copy[...] = block

    high, low = split(block)
    both = jnp.concatenate([high, low])
    high_acc[:half] += dot(both[:, :half], both, (0, 0))
    high_acc[half:, half:] += dot(both[:, half:], both[:, half:], (0, 0))
    mixed_acc[...] += dot(high, low, (0, 0))

    @pl.when(step == pl.num_programs(0) - 1)
    def _():
        for k, (i, j) in enumerate(block_pairs(high_acc.shape[0] // BLOCK)):
            rows, columns = pl.ds(i * BLOCK, BLOCK), pl.ds(j * BLOCK, BLOCK)
            mixed = mixed_acc[rows, columns] + mixed_acc[columns, rows].T
            g_ref[pl.ds(k * BLOCK, BLOCK), :] = (high_acc[rows, columns] + mixed) * scale


def own_gram(side, s, scale, spans):
    rows, width = s.shape
    square = (width, width)
    packed = (len(block_pairs(width // BLOCK)) * BLOCK, BLOCK)

    def copy_spec(start, shift, count):
        return pl.BlockSpec((TILE, width), lambda i, side: (jnp.clip(i - start - shift * side[0], 0, count - 1), 0))

    return pl.pallas_call(
        functools.partial(own_gram_kernel, scale, spans),
        grid_spec=pltpu.PrefetchScalarGridSpec(
            num_scalar_prefetch=1,
            grid=(rows // TILE,),
            in_specs=[pl.BlockSpec((TILE, width), lambda i, side: (i, 0))],
            out_specs=[pl.BlockSpec(packed, lambda i, side: (0, 0))] + [copy_spec(*span) for span in spans],
            scratch_shapes=[pltpu.VMEM(square, F32), pltpu.VMEM(square, F32)],
        ),
        out_shape=[jax.ShapeDtypeStruct(packed, F32)]
        + [jax.ShapeDtypeStruct((count * TILE, width), F32) for _, _, count in spans],
        compiler_params=params(60),
        cost_estimate=COST,
        name="own_gram",
    )(side, s)


def cross_gram_kernel(scale, resume, counts, side_ref, own_ref, *refs):
    chunks, before_ref, g_ref = refs[: len(counts)], refs[len(counts)], refs[-1]
    step = pl.program_id(0)
    first = side_ref[0] == 0

    @pl.when(step == 0)
    def _():
        g_ref[...] = before_ref[...] if resume else jnp.zeros_like(g_ref)

    begin = 0
    for chunk, count in zip(chunks, counts):

        @pl.when((step >= begin) & (step < begin + count))
        def _():
            own, other = own_ref[...], chunk[...]
            left = jnp.where(first, own, other)
            right = jnp.where(first, other, own)
            lh, ll = split(left)
            rh, rl = split(right * scale)
            left = jnp.concatenate([lh, ll, lh, ll])
            right = jnp.concatenate([rh, rl, rl, rh])
            g_ref[...] += dot(left, right, (0, 0))

        begin += count


def cross_gram(side, own, chunks, before, after, offset, scale):
    rows, width = own.shape
    counts = tuple(c.shape[0] // TILE for c in chunks)
    starts = [sum(counts[:i]) for i in range(len(counts))]
    square = (width, width)
    half = rows // 2 // TILE
    start = offset // TILE

    def chunk_spec(begin, count):
        return pl.BlockSpec((TILE, width), lambda i, side: (jnp.clip(i - begin, 0, count - 1), 0))

    in_specs = [pl.BlockSpec((TILE, width), lambda i, side: (i + start + (1 - side[0]) * half, 0))]
    in_specs += [chunk_spec(b, c) for b, c in zip(starts, counts)]
    in_specs += [pl.BlockSpec(square, lambda i, side: (0, 0))] * (before is not None)
    in_specs += [pl.BlockSpec(memory_space=pl.ANY)] * len(after)
    return pl.pallas_call(
        functools.partial(cross_gram_kernel, scale, before is not None, counts),
        grid_spec=pltpu.PrefetchScalarGridSpec(
            num_scalar_prefetch=1,
            grid=(sum(counts),),
            in_specs=in_specs,
            out_specs=pl.BlockSpec(square, lambda i, side: (0, 0)),
        ),
        out_shape=jax.ShapeDtypeStruct(square, F32),
        compiler_params=params(60),
        cost_estimate=COST,
        name="cross_gram",
    )(side, own, *chunks, *([] if before is None else [before]), *after)


def factor_block(a, x):
    count, width = len(a), a[0].shape[1]
    shape = (GROUP, width)
    row = lax.broadcasted_iota(jnp.int32, shape, 0)
    lane = lax.broadcasted_iota(jnp.int32, shape, 1)
    upper, inverse = [], []
    for p in range(count):
        c = GROUP * p
        pa = [jnp.broadcast_to(a[p][k : k + 1, :], shape) for k in range(GROUP)]
        px = [jnp.broadcast_to(x[p][k : k + 1, :], shape) for k in range(GROUP)]
        s = [
            [jnp.broadcast_to(pa[k][:, c + l : c + l + 1], shape) if l >= k else None for l in range(GROUP)]
            for k in range(GROUP)
        ]
        reciprocal = []
        for k in range(GROUP):
            reciprocal.append(1.0 / s[k][k])
            for l in range(k + 1, GROUP):
                m = s[k][l] * reciprocal[k]
                for t in range(l, GROUP):
                    s[l][t] = s[l][t] - m * s[k][t]
                pa[l] = pa[l] - m * pa[k]
                px[l] = px[l] - m * px[k]
        for r in range(p + 1, count):
            columns = [jnp.broadcast_to(a[r][:, c + l : c + l + 1], shape) for l in range(GROUP)]
            for k in range(GROUP):
                m = columns[k] * reciprocal[k]
                for t in range(k + 1, GROUP):
                    columns[t] = columns[t] - m * s[k][t]
                a[r] = a[r] - m * pa[k]
                x[r] = x[r] - m * px[k]
        ua, ux = None, None
        for k in range(GROUP):
            root = lax.rsqrt(s[k][k])
            va, vx = pa[k] * root, px[k] * root
            ua = va if k == 0 else jnp.where(row == k, va, ua)
            ux = vx if k == 0 else jnp.where(row == k, vx, ux)
        upper.append(jnp.where(lane >= row + c, ua, 0.0))
        inverse.append(ux)
    return upper, inverse


def factor_whole(a_ref, r_ref, x_ref, e_ref, beside=None):
    order = a_ref.shape[0]
    blocks = order // BLOCK
    groups = BLOCK // GROUP
    r_ref[...] = jnp.zeros_like(r_ref)
    x_ref[...] = jnp.zeros_like(x_ref)
    row = lax.broadcasted_iota(jnp.int32, (GROUP, BLOCK), 0)
    lane = lax.broadcasted_iota(jnp.int32, (GROUP, BLOCK), 1)

    def body(b, carry):
        start = pl.multiple_of(b * BLOCK, BLOCK)
        here = pl.ds(start, BLOCK)
        a = [a_ref[pl.ds(start + GROUP * i, GROUP), here] for i in range(groups)]
        x = [jnp.where(lane == row + GROUP * i, 1.0, 0.0) for i in range(groups)]
        if beside is not None:
            beside(b, blocks)
        upper, inverse = factor_block(a, x)
        for i in range(groups):
            r_ref[pl.ds(start + GROUP * i, GROUP), here] = upper[i]
            e_ref[pl.ds(GROUP * i, GROUP), :] = inverse[i]
        for k in range(blocks):

            @pl.when(b == k)
            def _():
                lo, hi = k * BLOCK, (k + 1) * BLOCK
                e = e_ref[...]
                x_ref[lo:hi, lo:hi] = e
                if k > 0:
                    x_ref[lo:hi, :lo] = dot(e, x_ref[lo:hi, :lo], (1, 0), HIGHEST)
                if hi < order:
                    strip = dot(e, a_ref[lo:hi, hi:], (1, 0), HIGHEST)
                    r_ref[lo:hi, hi:] = strip
                    a_ref[hi:, hi:] -= dot(strip, strip, (0, 0), HIGHEST)
                    x_ref[hi:, :hi] -= dot(strip, x_ref[lo:hi, :hi], (0, 0), HIGHEST)

        return carry

    lax.fori_loop(0, blocks, body, 0)


def unpack(packed_ref, a_ref):
    for k, (i, j) in enumerate(block_pairs(a_ref.shape[0] // BLOCK)):
        a_ref[pl.ds(i * BLOCK, BLOCK), pl.ds(j * BLOCK, BLOCK)] = packed_ref[pl.ds(k * BLOCK, BLOCK), :]


def first_factor_kernel(g_ref, r_ref, x_ref, a_ref, e_ref):
    unpack(g_ref, a_ref)
    factor_whole(a_ref, r_ref, x_ref, e_ref)


def first_factor(packed, order):
    square = jax.ShapeDtypeStruct((order, order), F32)
    return pl.pallas_call(
        first_factor_kernel,
        out_shape=[square, square],
        in_specs=whole(1),
        out_specs=whole(2),
        scratch_shapes=[pltpu.VMEM((order, order), F32), pltpu.VMEM((BLOCK, BLOCK), F32)],
        compiler_params=params(40),
        cost_estimate=COST,
        name="first_factor",
    )(packed)


def thrice(x):
    high, low = split(x)
    return jnp.concatenate([high, high, low], axis=1)


def stacked(w):
    high, low = split(w)
    return jnp.concatenate([high, low, high], axis=0)


def times_upper(x, left, right):
    half = x.shape[1] // 2
    return jnp.concatenate(
        [dot(thrice(x[:, :half]), left, (1, 0)), dot(thrice(x), right, (1, 0))], axis=1
    )


def finish_kernel(counts, side_ref, cross_ref, g_ref, r00_ref, x0_ref, own_hbm, *refs):
    chunks, refs = refs[: len(counts)], refs[len(counts) :]
    f_ref, factor_ref, part_ref, basis_hbm = refs[:4]
    own, other, u_ref, left_ref, right_ref, a_ref, r_ref, x_ref, e_ref, load_sems, store_sems = refs[4:]
    order = a_ref.shape[0]
    half = order // 2
    rows, known = own.shape[0], sum(counts)
    first = side_ref[0] == 0
    loads = [pltpu.make_async_copy(own_hbm, own, load_sems.at[len(counts)])]
    begin = 0
    for k, count in enumerate(counts):
        loads.append(pltpu.make_async_copy(chunks[k], other.at[pl.ds(begin, count)], load_sems.at[k]))
        begin += count
    for load in loads:
        load.start()
    x0 = x0_ref[...]
    r01 = dot(x0, cross_ref[...], (1, 0), HIGHEST)
    u = dot3(x0, r01, (0, 0))
    u_ref[...] = stacked(jnp.where(first, 0.0, u))
    unpack(g_ref, a_ref)
    a_ref[...] -= dot(r01, r01, (0, 0), HIGHEST)
    f_ref[:order] = jnp.where(first, r00_ref[...], r01)
    for load in loads:
        load.wait()

    def project(b, blocks):
        size = other.shape[0] // blocks
        tile = math.gcd(size, TILE)
        for k in range(size // tile):
            here = pl.ds(pl.multiple_of(b * size + k * tile, tile), tile)
            own[here] -= dot(thrice(other[here]), u_ref[...], (1, 0))

    factor_whole(a_ref, r_ref, x_ref, e_ref, project)
    x1 = x_ref[...]
    w = jnp.where(first, x0, x1).T
    left_ref[...] = stacked(w[:half, :half])
    right_ref[...] = stacked(w[:, half:])

    def store(k):
        here = pl.ds(pl.multiple_of(k * TILE, TILE), TILE)
        return pltpu.make_async_copy(own.at[here], basis_hbm.at[here], store_sems.at[k])

    def body(k, carry):
        here = pl.ds(pl.multiple_of(k * TILE, TILE), TILE)
        own[here] = times_upper(own[here], left_ref[...], right_ref[...])
        store(k).start()
        return carry

    lax.fori_loop(0, known // TILE, body, 0)
    for k in range(known, rows, TILE):
        part_ref[k - known : k - known + TILE] = times_upper(own[k : k + TILE], left_ref[...], right_ref[...])
    f_ref[order:] = jnp.where(first, 0.0, r_ref[...])
    factor_ref[...] = stacked(jnp.where(first, 0.0, -dot3(u, x1, (1, 1))))
    for k in range(known // TILE):
        store(k).wait()


def finish(side, cross, packed, r00, x0, own, chunks):
    order = cross.shape[0]
    half = order // 2
    square = (order, order)
    counts = tuple(c.shape[0] for c in chunks)
    anywhere = pl.BlockSpec(memory_space=pltpu.HBM)
    return pl.pallas_call(
        functools.partial(finish_kernel, counts),
        out_shape=[
            jax.ShapeDtypeStruct((2 * order, order), F32),
            jax.ShapeDtypeStruct((3 * order, order), BF16),
            jax.ShapeDtypeStruct((own.shape[0] - sum(counts), order), F32),
            jax.ShapeDtypeStruct(own.shape, F32),
        ],
        in_specs=[pl.BlockSpec(memory_space=pltpu.SMEM)] + whole(4) + [anywhere] * (1 + len(chunks)),
        out_specs=whole(3) + [anywhere],
        scratch_shapes=[
            pltpu.VMEM(own.shape, F32),
            pltpu.VMEM((sum(counts), order), F32),
            pltpu.VMEM((3 * order, order), BF16),
            pltpu.VMEM((3 * half, half), BF16),
            pltpu.VMEM((3 * order, half), BF16),
            pltpu.VMEM(square, F32),
            pltpu.VMEM(square, F32),
            pltpu.VMEM(square, F32),
            pltpu.VMEM((BLOCK, BLOCK), F32),
            pltpu.SemaphoreType.DMA((len(chunks) + 1,)),
            pltpu.SemaphoreType.DMA((sum(counts) // TILE,)),
        ],
        compiler_params=params(60),
        cost_estimate=COST,
        name="finish",
    )(side, cross, packed, r00, x0, own, *chunks)


def tail_kernel(start, row, chunk_ref, factor_ref, part_ref, before_hbm, basis_hbm, out, sems):
    copies = []
    for k in range(out.shape[0]):
        size = out.shape[1]
        here = pl.ds(k * size, size)
        out[k] = part_ref[pl.ds(start + k * size, size)] + dot(thrice(chunk_ref[here]), factor_ref[...], (1, 0))
        copies.append(pltpu.make_async_copy(out.at[k], basis_hbm.at[pl.ds(row + k * size, size)], sems.at[k]))
        copies[-1].start()
    for copy in copies:
        copy.wait()


def tail(chunk, factor, part, start, row, basis):
    rows, width = chunk.shape
    tile = math.gcd(TILE // 2, rows)
    anywhere = pl.BlockSpec(memory_space=pltpu.HBM)
    return pl.pallas_call(
        functools.partial(tail_kernel, start, row),
        in_specs=whole(3) + [anywhere],
        out_specs=anywhere,
        out_shape=jax.ShapeDtypeStruct(basis.shape, F32),
        scratch_shapes=[pltpu.VMEM((rows // tile, tile, width), F32), pltpu.SemaphoreType.DMA((rows // tile,))],
        input_output_aliases={3: 0},
        compiler_params=params(12),
        cost_estimate=COST,
        name="tail",
    )(chunk, factor, part, basis)


def flip(x, order, step):
    count = lax.axis_size("dof")
    return lax.ppermute(x, "dof", [(i, i ^ order[i % 2][step]) for i in range(count)])


def flip_side(x, order, sides):
    count = lax.axis_size("dof")
    pairs = [(2 * i + j, 2 * (i ^ order[i % 2][-1]) + 1 - j) for i in range(count) for j in sides]
    return lax.ppermute(x, ("dof", "snap"), pairs)


def halve(x, upper, send):
    half = x.shape[0] // 2
    low, high = x[:half], x[half:]
    return jnp.where(upper, high, low) + send(jnp.where(upper, low, high))


def double_with(x, other, upper, axis=0):
    return jnp.concatenate([jnp.where(upper, other, x), jnp.where(upper, x, other)], axis)


def double(x, upper, send, axis=0):
    return double_with(x, send(x), upper, axis)


def on_device(snapshots):
    rows, width = snapshots.shape
    count = lax.axis_size("dof")
    scale = 1.0 / (rows * count)
    me, side = lax.axis_index("dof"), lax.axis_index("snap")
    side_operand = jnp.full((1,), side, jnp.int32)
    bits = [1 << i for i in range(1, count.bit_length() - 1)]
    order = ([1] + bits[1:] + bits[:1], [1] + bits)
    steps = list(range(len(order[0])))

    def bit(step):
        return (me & jnp.where(me % 2 == 0, order[0][step], order[1][step])) != 0

    def send(step):
        return lambda x: flip(x, order, step)

    def reduce_own(i, carry):
        shard = carry[0]
        for k in steps:
            shard = halve(shard, bit(k), send(k))
        received = flip_side(shard, order, (0, 1))
        upper = bit(steps[-1]) ^ (side == 1)
        first = jnp.where(side == 0, shard, received)
        second = jnp.where(side == 0, received, shard)
        first = double(first, upper, send(steps[-1]))
        second = double(second, ~upper, send(steps[-1]))
        for k in steps[-2::-1]:
            first = double(first, bit(k), send(k))
            second = double(second, bit(k), send(k))
        return first, second

    def reduce_cross(i, cross):
        for k in steps[:-1]:
            cross = halve(cross, bit(k), send(k))
        cross = cross + flip_side(cross, order, (0,))
        cross = cross + send(steps[-1])(cross)
        for k in steps[-2::-1]:
            cross = double(cross, bit(k), send(k))
        return cross

    half = rows // 2 // TILE
    parts = [half // 4, half // 2, half - half // 4 - half // 2]
    rests = [half // 2, half - half // 2]
    spans = [(parts[0], half, parts[1]), (parts[0] + parts[1], half, parts[2])]
    spans += [(half + sum(rests[:i]), 0, rests[i]) for i in range(2)]

    def swap(x):
        return lax.ppermute(x, "snap", [(0, 1), (1, 0)])

    def one_way(x):
        return lax.ppermute(x, "snap", [(0, 1)])

    def late(x, after):
        return lax.optimization_barrier((x, after))[0]

    once = 1 + jnp.minimum(side, 0)
    arrived = [swap(lax.dynamic_slice_in_dim(snapshots, side * half * TILE, parts[0] * TILE, 0))]
    own, *sends = own_gram(side_operand, snapshots, scale, spans)
    arrived.append(swap(sends[0]))
    first, second = lax.fori_loop(0, once, reduce_own, (own, own))
    arrived.append(swap(late(sends[1], first)))
    r00, x00 = first_factor(first, width)
    arrived.append(one_way(late(sends[2], r00)))
    early = parts[0] + parts[1]
    cross = cross_gram(side_operand, snapshots, arrived[:2], None, [x00, second], 0, scale)
    arrived.append(one_way(late(sends[3], cross)))
    cross = cross_gram(side_operand, snapshots, arrived[2:3], cross, [], early * TILE, scale)
    cross = lax.fori_loop(0, once, reduce_cross, cross)
    factor, share, part, basis = finish(side_operand, cross, second, r00, x00, snapshots, arrived[:4])
    begin = half + rests[0]
    basis = tail(arrived[4], share, part, 0, begin * TILE, basis)
    return (basis, factor)


def solution(mesh):
    in_specs = (P("dof", "snap"),)
    out_specs = (P("dof", "snap"), P(None, "snap"))
    return jax.shard_map(
        on_device, mesh=mesh, in_specs=in_specs, out_specs=out_specs, check_vma=False
    )
```

```python
import functools
import math

import jax
import jax.numpy as jnp
from jax import lax
from jax.experimental import pallas as pl
from jax.experimental.pallas import tpu as pltpu
from jax.sharding import PartitionSpec as P

F32 = jnp.float32
BF16 = jnp.bfloat16
HIGHEST = lax.Precision.HIGHEST
VMEM = pltpu.VMEM
BLOCK = 128
GROUP = 8
TILE = 512
COST = pl.CostEstimate(flops=1, bytes_accessed=1, transcendentals=0)


def params(megabytes):
    return pltpu.CompilerParams(vmem_limit_bytes=megabytes * 1024 * 1024)


def whole(count):
    return [pl.BlockSpec(memory_space=VMEM)] * count


def dot(a, b, contract, precision=None):
    return lax.dot_general(
        a, b, ((contract[:1], contract[1:]), ((), ())), precision=precision, preferred_element_type=F32
    )


def split(x):
    high = x.astype(BF16)
    return high, (x - high.astype(F32)).astype(BF16)


def dot3(a, b, contract):
    ah, al = split(a)
    bh, bl = split(b)
    return dot(ah, bh, contract) + (dot(ah, bl, contract) + dot(al, bh, contract))


def pick_kernel(starts, side_ref, s_hbm, out_hbm, buffer, in_sems, out_sems):
    count, rows = buffer.shape[:2]
    start = pl.multiple_of(jnp.where(side_ref[0] == 0, starts[0], starts[1]), TILE)
    ins, outs = [], []
    for k in range(count):
        here = pl.ds(k * rows, rows)
        ins.append(pltpu.make_async_copy(s_hbm.at[pl.ds(start + k * rows, rows)], buffer.at[k], in_sems.at[k]))
        outs.append(pltpu.make_async_copy(buffer.at[k], out_hbm.at[here], out_sems.at[k]))
    for copy in ins:
        copy.start()
    for before, after in zip(ins, outs):
        before.wait()
        after.start()
    for copy in outs:
        copy.wait()


def pick(side, s, starts, rows):
    hbm = pl.BlockSpec(memory_space=pltpu.HBM)
    return pl.pallas_call(
        functools.partial(pick_kernel, starts),
        in_specs=[pl.BlockSpec(memory_space=pltpu.SMEM), hbm],
        out_specs=hbm,
        out_shape=jax.ShapeDtypeStruct((rows, s.shape[1]), F32),
        scratch_shapes=[
            pltpu.VMEM((4, rows // 4, s.shape[1]), F32),
            pltpu.SemaphoreType.DMA((4,)),
            pltpu.SemaphoreType.DMA((4,)),
        ],
        compiler_params=params(60),
        cost_estimate=COST,
        name="pick",
    )(side, s)


def block_pairs(blocks):
    return [(i, j) for i in range(blocks) for j in range(i, blocks)]


def own_gram_kernel(scale, spans, side_ref, s_ref, g_ref, *refs):
    copies, (high_acc, mixed_acc) = refs[:-2], refs[-2:]
    step = pl.program_id(0)
    half = high_acc.shape[0] // 2

    @pl.when(step == 0)
    def _():
        high_acc[...] = jnp.zeros_like(high_acc)
        mixed_acc[...] = jnp.zeros_like(mixed_acc)

    block = s_ref[...]
    for copy, (start, shift, count) in zip(copies, spans):
        begin = start + shift * side_ref[0]

        @pl.when((step >= begin) & (step < begin + count))
        def _():
            copy[...] = block

    high, low = split(block)
    both = jnp.concatenate([high, low])
    high_acc[:half] += dot(both[:, :half], both, (0, 0))
    high_acc[half:, half:] += dot(both[:, half:], both[:, half:], (0, 0))
    mixed_acc[...] += dot(high, low, (0, 0))

    @pl.when(step == pl.num_programs(0) - 1)
    def _():
        for k, (i, j) in enumerate(block_pairs(high_acc.shape[0] // BLOCK)):
            rows, columns = pl.ds(i * BLOCK, BLOCK), pl.ds(j * BLOCK, BLOCK)
            mixed = mixed_acc[rows, columns] + mixed_acc[columns, rows].T
            g_ref[pl.ds(k * BLOCK, BLOCK), :] = (high_acc[rows, columns] + mixed) * scale


def own_gram(side, s, scale, spans):
    rows, width = s.shape
    square = (width, width)
    packed = (len(block_pairs(width // BLOCK)) * BLOCK, BLOCK)

    def copy_spec(start, shift, count):
        return pl.BlockSpec((TILE, width), lambda i, side: (jnp.clip(i - start - shift * side[0], 0, count - 1), 0))

    return pl.pallas_call(
        functools.partial(own_gram_kernel, scale, spans),
        grid_spec=pltpu.PrefetchScalarGridSpec(
            num_scalar_prefetch=1,
            grid=(rows // TILE,),
            in_specs=[pl.BlockSpec((TILE, width), lambda i, side: (i, 0))],
            out_specs=[pl.BlockSpec(packed, lambda i, side: (0, 0))] + [copy_spec(*span) for span in spans],
            scratch_shapes=[pltpu.VMEM(square, F32), pltpu.VMEM(square, F32)],
        ),
        out_shape=[jax.ShapeDtypeStruct(packed, F32)]
        + [jax.ShapeDtypeStruct((count * TILE, width), F32) for _, _, count in spans],
        compiler_params=params(60),
        cost_estimate=COST,
        name="own_gram",
    )(side, s)


def cross_gram_kernel(scale, resume, counts, side_ref, own_ref, *refs):
    chunks, before_ref, g_ref = refs[: len(counts)], refs[len(counts)], refs[-1]
    step = pl.program_id(0)
    first = side_ref[0] == 0

    @pl.when(step == 0)
    def _():
        g_ref[...] = before_ref[...] if resume else jnp.zeros_like(g_ref)

    begin = 0
    for chunk, count in zip(chunks, counts):

        @pl.when((step >= begin) & (step < begin + count))
        def _():
            own, other = own_ref[...], chunk[...]
            left = jnp.where(first, own, other)
            right = jnp.where(first, other, own)
            lh, ll = split(left)
            rh, rl = split(right * scale)
            left = jnp.concatenate([lh, ll, lh, ll])
            right = jnp.concatenate([rh, rl, rl, rh])
            g_ref[...] += dot(left, right, (0, 0))

        begin += count


def cross_gram(side, own, chunks, before, after, offset, scale):
    rows, width = own.shape
    counts = tuple(c.shape[0] // TILE for c in chunks)
    starts = [sum(counts[:i]) for i in range(len(counts))]
    square = (width, width)
    half = rows // 2 // TILE
    start = offset // TILE

    def chunk_spec(begin, count):
        return pl.BlockSpec((TILE, width), lambda i, side: (jnp.clip(i - begin, 0, count - 1), 0))

    in_specs = [pl.BlockSpec((TILE, width), lambda i, side: (i + start + (1 - side[0]) * half, 0))]
    in_specs += [chunk_spec(b, c) for b, c in zip(starts, counts)]
    in_specs += [pl.BlockSpec(square, lambda i, side: (0, 0))] * (before is not None)
    in_specs += [pl.BlockSpec(memory_space=pl.ANY)] * len(after)
    return pl.pallas_call(
        functools.partial(cross_gram_kernel, scale, before is not None, counts),
        grid_spec=pltpu.PrefetchScalarGridSpec(
            num_scalar_prefetch=1,
            grid=(sum(counts),),
            in_specs=in_specs,
            out_specs=pl.BlockSpec(square, lambda i, side: (0, 0)),
        ),
        out_shape=jax.ShapeDtypeStruct(square, F32),
        compiler_params=params(60),
        cost_estimate=COST,
        name="cross_gram",
    )(side, own, *chunks, *([] if before is None else [before]), *after)


def factor_block(a, x):
    count, width = len(a), a[0].shape[1]
    shape = (GROUP, width)
    row = lax.broadcasted_iota(jnp.int32, shape, 0)
    lane = lax.broadcasted_iota(jnp.int32, shape, 1)
    upper, inverse = [], []
    for p in range(count):
        c = GROUP * p
        pa = [jnp.broadcast_to(a[p][k : k + 1, :], shape) for k in range(GROUP)]
        px = [jnp.broadcast_to(x[p][k : k + 1, :], shape) for k in range(GROUP)]
        s = [
            [jnp.broadcast_to(pa[k][:, c + l : c + l + 1], shape) if l >= k else None for l in range(GROUP)]
            for k in range(GROUP)
        ]
        reciprocal = []
        for k in range(GROUP):
            reciprocal.append(1.0 / s[k][k])
            for l in range(k + 1, GROUP):
                m = s[k][l] * reciprocal[k]
                for t in range(l, GROUP):
                    s[l][t] = s[l][t] - m * s[k][t]
                pa[l] = pa[l] - m * pa[k]
                px[l] = px[l] - m * px[k]
        for r in range(p + 1, count):
            columns = [jnp.broadcast_to(a[r][:, c + l : c + l + 1], shape) for l in range(GROUP)]
            for k in range(GROUP):
                m = columns[k] * reciprocal[k]
                for t in range(k + 1, GROUP):
                    columns[t] = columns[t] - m * s[k][t]
                a[r] = a[r] - m * pa[k]
                x[r] = x[r] - m * px[k]
        ua, ux = None, None
        for k in range(GROUP):
            root = lax.rsqrt(s[k][k])
            va, vx = pa[k] * root, px[k] * root
            ua = va if k == 0 else jnp.where(row == k, va, ua)
            ux = vx if k == 0 else jnp.where(row == k, vx, ux)
        upper.append(jnp.where(lane >= row + c, ua, 0.0))
        inverse.append(ux)
    return upper, inverse


def factor_whole(a_ref, r_ref, x_ref, e_ref, beside=None):
    order = a_ref.shape[0]
    blocks = order // BLOCK
    groups = BLOCK // GROUP
    r_ref[...] = jnp.zeros_like(r_ref)
    x_ref[...] = jnp.zeros_like(x_ref)
    row = lax.broadcasted_iota(jnp.int32, (GROUP, BLOCK), 0)
    lane = lax.broadcasted_iota(jnp.int32, (GROUP, BLOCK), 1)

    def body(b, carry):
        start = pl.multiple_of(b * BLOCK, BLOCK)
        here = pl.ds(start, BLOCK)
        a = [a_ref[pl.ds(start + GROUP * i, GROUP), here] for i in range(groups)]
        x = [jnp.where(lane == row + GROUP * i, 1.0, 0.0) for i in range(groups)]
        if beside is not None:
            beside(b, blocks)
        upper, inverse = factor_block(a, x)
        for i in range(groups):
            r_ref[pl.ds(start + GROUP * i, GROUP), here] = upper[i]
            e_ref[pl.ds(GROUP * i, GROUP), :] = inverse[i]
        for k in range(blocks):

            @pl.when(b == k)
            def _():
                lo, hi = k * BLOCK, (k + 1) * BLOCK
                e = e_ref[...]
                x_ref[lo:hi, lo:hi] = e
                if k > 0:
                    x_ref[lo:hi, :lo] = dot(e, x_ref[lo:hi, :lo], (1, 0), HIGHEST)
                if hi < order:
                    strip = dot(e, a_ref[lo:hi, hi:], (1, 0), HIGHEST)
                    r_ref[lo:hi, hi:] = strip
                    a_ref[hi:, hi:] -= dot(strip, strip, (0, 0), HIGHEST)
                    x_ref[hi:, :hi] -= dot(strip, x_ref[lo:hi, :hi], (0, 0), HIGHEST)

        return carry

    lax.fori_loop(0, blocks, body, 0)


def unpack(packed_ref, a_ref):
    for k, (i, j) in enumerate(block_pairs(a_ref.shape[0] // BLOCK)):
        a_ref[pl.ds(i * BLOCK, BLOCK), pl.ds(j * BLOCK, BLOCK)] = packed_ref[pl.ds(k * BLOCK, BLOCK), :]


def first_factor_kernel(g_ref, r_ref, x_ref, a_ref, e_ref):
    unpack(g_ref, a_ref)
    factor_whole(a_ref, r_ref, x_ref, e_ref)


def first_factor(packed, order):
    square = jax.ShapeDtypeStruct((order, order), F32)
    return pl.pallas_call(
        first_factor_kernel,
        out_shape=[square, square],
        in_specs=whole(1),
        out_specs=whole(2),
        scratch_shapes=[pltpu.VMEM((order, order), F32), pltpu.VMEM((BLOCK, BLOCK), F32)],
        compiler_params=params(40),
        cost_estimate=COST,
        name="first_factor",
    )(packed)


def thrice(x):
    high, low = split(x)
    return jnp.concatenate([high, high, low], axis=1)


def stacked(w):
    high, low = split(w)
    return jnp.concatenate([high, low, high], axis=0)


def times_upper(x, left, right):
    half = x.shape[1] // 2
    return jnp.concatenate(
        [dot(thrice(x[:, :half]), left, (1, 0)), dot(thrice(x), right, (1, 0))], axis=1
    )


def finish_kernel(counts, side_ref, cross_ref, g_ref, r00_ref, x0_ref, own_hbm, *refs):
    chunks, refs = refs[: len(counts)], refs[len(counts) :]
    f_ref, factor_ref, part_ref, basis_hbm = refs[:4]
    own, other, u_ref, left_ref, right_ref, a_ref, r_ref, x_ref, e_ref, load_sems, store_sems = refs[4:]
    order = a_ref.shape[0]
    half = order // 2
    rows, known = own.shape[0], sum(counts)
    first = side_ref[0] == 0
    loads = [pltpu.make_async_copy(own_hbm, own, load_sems.at[len(counts)])]
    begin = 0
    for k, count in enumerate(counts):
        loads.append(pltpu.make_async_copy(chunks[k], other.at[pl.ds(begin, count)], load_sems.at[k]))
        begin += count
    for load in loads:
        load.start()
    x0 = x0_ref[...]
    r01 = dot(x0, cross_ref[...], (1, 0), HIGHEST)
    u = dot3(x0, r01, (0, 0))
    u_ref[...] = stacked(jnp.where(first, 0.0, u))
    unpack(g_ref, a_ref)
    a_ref[...] -= dot(r01, r01, (0, 0), HIGHEST)
    f_ref[:order] = jnp.where(first, r00_ref[...], r01)
    for load in loads:
        load.wait()

    def project(b, blocks):
        size = other.shape[0] // blocks
        tile = math.gcd(size, TILE)
        for k in range(size // tile):
            here = pl.ds(pl.multiple_of(b * size + k * tile, tile), tile)
            own[here] -= dot(thrice(other[here]), u_ref[...], (1, 0))

    factor_whole(a_ref, r_ref, x_ref, e_ref, project)
    x1 = x_ref[...]
    w = jnp.where(first, x0, x1).T
    left_ref[...] = stacked(w[:half, :half])
    right_ref[...] = stacked(w[:, half:])

    def store(k):
        here = pl.ds(pl.multiple_of(k * TILE, TILE), TILE)
        return pltpu.make_async_copy(own.at[here], basis_hbm.at[here], store_sems.at[k])

    def body(k, carry):
        here = pl.ds(pl.multiple_of(k * TILE, TILE), TILE)
        own[here] = times_upper(own[here], left_ref[...], right_ref[...])
        store(k).start()
        return carry

    lax.fori_loop(0, known // TILE, body, 0)
    for k in range(known, rows, TILE):
        part_ref[k - known : k - known + TILE] = times_upper(own[k : k + TILE], left_ref[...], right_ref[...])
    f_ref[order:] = jnp.where(first, 0.0, r_ref[...])
    factor_ref[...] = stacked(jnp.where(first, 0.0, -dot3(u, x1, (1, 1))))
    for k in range(known // TILE):
        store(k).wait()


def finish(side, cross, packed, r00, x0, own, chunks):
    order = cross.shape[0]
    half = order // 2
    square = (order, order)
    counts = tuple(c.shape[0] for c in chunks)
    anywhere = pl.BlockSpec(memory_space=pltpu.HBM)
    return pl.pallas_call(
        functools.partial(finish_kernel, counts),
        out_shape=[
            jax.ShapeDtypeStruct((2 * order, order), F32),
            jax.ShapeDtypeStruct((3 * order, order), BF16),
            jax.ShapeDtypeStruct((own.shape[0] - sum(counts), order), F32),
            jax.ShapeDtypeStruct(own.shape, F32),
        ],
        in_specs=[pl.BlockSpec(memory_space=pltpu.SMEM)] + whole(4) + [anywhere] * (1 + len(chunks)),
        out_specs=whole(3) + [anywhere],
        scratch_shapes=[
            pltpu.VMEM(own.shape, F32),
            pltpu.VMEM((sum(counts), order), F32),
            pltpu.VMEM((3 * order, order), BF16),
            pltpu.VMEM((3 * half, half), BF16),
            pltpu.VMEM((3 * order, half), BF16),
            pltpu.VMEM(square, F32),
            pltpu.VMEM(square, F32),
            pltpu.VMEM(square, F32),
            pltpu.VMEM((BLOCK, BLOCK), F32),
            pltpu.SemaphoreType.DMA((len(chunks) + 1,)),
            pltpu.SemaphoreType.DMA((sum(counts) // TILE,)),
        ],
        compiler_params=params(60),
        cost_estimate=COST,
        name="finish",
    )(side, cross, packed, r00, x0, own, *chunks)


def stage_kernel(factor_ref, part_ref, factor_out, part_out):
    factor_out[...] = factor_ref[...]
    part_out[...] = part_ref[...]


def stage(factor, part):
    return pl.pallas_call(
        stage_kernel,
        in_specs=whole(2),
        out_specs=whole(2),
        out_shape=[jax.ShapeDtypeStruct(factor.shape, BF16), jax.ShapeDtypeStruct(part.shape, F32)],
        compiler_params=params(12),
        cost_estimate=COST,
        name="stage",
    )(factor, part)


def tail_kernel(start, row, chunk_ref, factor_ref, part_ref, before_hbm, basis_hbm, out, sems):
    copies = []
    for k in range(out.shape[0]):
        size = out.shape[1]
        here = pl.ds(k * size, size)
        out[k] = part_ref[pl.ds(start + k * size, size)] + dot(thrice(chunk_ref[here]), factor_ref[...], (1, 0))
        copies.append(pltpu.make_async_copy(out.at[k], basis_hbm.at[pl.ds(row + k * size, size)], sems.at[k]))
        copies[-1].start()
    for copy in copies:
        copy.wait()


def tail(chunk, factor, part, start, row, basis):
    rows, width = chunk.shape
    tile = math.gcd(TILE // 2, rows)
    anywhere = pl.BlockSpec(memory_space=pltpu.HBM)
    return pl.pallas_call(
        functools.partial(tail_kernel, start, row),
        in_specs=whole(3) + [anywhere],
        out_specs=anywhere,
        out_shape=jax.ShapeDtypeStruct(basis.shape, F32),
        scratch_shapes=[pltpu.VMEM((rows // tile, tile, width), F32), pltpu.SemaphoreType.DMA((rows // tile,))],
        input_output_aliases={3: 0},
        compiler_params=params(12),
        cost_estimate=COST,
        name="tail",
    )(chunk, factor, part, basis)


def flip(x, order, step):
    count = lax.axis_size("dof")
    return lax.ppermute(x, "dof", [(i, i ^ order[i % 2][step]) for i in range(count)])


def flip_side(x, order, sides):
    count = lax.axis_size("dof")
    pairs = [(2 * i + j, 2 * (i ^ order[i % 2][-1]) + 1 - j) for i in range(count) for j in sides]
    return lax.ppermute(x, ("dof", "snap"), pairs)


def halve(x, upper, send):
    half = x.shape[0] // 2
    low, high = x[:half], x[half:]
    return jnp.where(upper, high, low) + send(jnp.where(upper, low, high))


def double_with(x, other, upper, axis=0):
    return jnp.concatenate([jnp.where(upper, other, x), jnp.where(upper, x, other)], axis)


def double(x, upper, send, axis=0):
    return double_with(x, send(x), upper, axis)


def on_device(snapshots):
    rows, width = snapshots.shape
    count = lax.axis_size("dof")
    scale = 1.0 / (rows * count)
    me, side = lax.axis_index("dof"), lax.axis_index("snap")
    side_operand = jnp.full((1,), side, jnp.int32)
    bits = [1 << i for i in range(1, count.bit_length() - 1)]
    order = ([1] + bits[1:] + bits[:1], [1] + bits)
    steps = list(range(len(order[0])))

    def bit(step):
        return (me & jnp.where(me % 2 == 0, order[0][step], order[1][step])) != 0

    def send(step):
        return lambda x: flip(x, order, step)

    def reduce_own(i, carry):
        shard = carry[0]
        for k in steps:
            shard = halve(shard, bit(k), send(k))
        received = flip_side(shard, order, (0, 1))
        upper = bit(steps[-1]) ^ (side == 1)
        first = jnp.where(side == 0, shard, received)
        second = jnp.where(side == 0, received, shard)
        first = double(first, upper, send(steps[-1]))
        second = double(second, ~upper, send(steps[-1]))
        for k in steps[-2::-1]:
            first = double(first, bit(k), send(k))
            second = double(second, bit(k), send(k))
        return first, second

    def reduce_cross(i, cross):
        for k in steps[:-1]:
            cross = halve(cross, bit(k), send(k))
        cross = cross + flip_side(cross, order, (0,))
        cross = cross + send(steps[-1])(cross)
        for k in steps[-2::-1]:
            cross = double(cross, bit(k), send(k))
        return cross

    half = rows // 2 // TILE
    parts = [half // 4, half // 2, half - half // 4 - half // 2]
    rests = [half // 2, half - half // 2]
    spans = [(parts[0], half, parts[1]), (parts[0] + parts[1], half, parts[2])]
    spans += [(half + sum(rests[:i]), 0, rests[i]) for i in range(2)]

    def swap(x):
        return lax.ppermute(x, "snap", [(0, 1), (1, 0)])

    def one_way(x):
        return lax.ppermute(x, "snap", [(0, 1)])

    def late(x, after):
        return lax.optimization_barrier((x, after))[0]

    once = 1 + jnp.minimum(side, 0)
    arrived = [swap(pick(side_operand, snapshots, (0, half * TILE), parts[0] * TILE))]
    own, *sends = own_gram(side_operand, snapshots, scale, spans)
    arrived.append(swap(sends[0]))
    first, second = lax.fori_loop(0, once, reduce_own, (own, own))
    arrived.append(swap(late(sends[1], first)))
    r00, x00 = first_factor(first, width)
    arrived.append(one_way(late(sends[2], r00)))
    early = parts[0] + parts[1]
    cross = cross_gram(side_operand, snapshots, arrived[:2], None, [x00, second], 0, scale)
    arrived.append(one_way(late(sends[3], cross)))
    cross = cross_gram(side_operand, snapshots, arrived[2:3], cross, [], early * TILE, scale)
    cross = lax.fori_loop(0, once, reduce_cross, cross)
    factor, share, part, basis = finish(side_operand, cross, second, r00, x00, snapshots, arrived[:4])
    share, part = stage(share, part)
    begin = half + rests[0]
    basis = tail(arrived[4], share, part, 0, begin * TILE, basis)
    return (basis, factor)


def solution(mesh):
    in_specs = (P("dof", "snap"),)
    out_specs = (P("dof", "snap"), P(None, "snap"))
    return jax.shard_map(
        on_device, mesh=mesh, in_specs=in_specs, out_specs=out_specs, check_vma=False
    )
```

```python
import functools
import math

import jax
import jax.numpy as jnp
from jax import lax
from jax.experimental import pallas as pl
from jax.experimental.pallas import tpu as pltpu
from jax.sharding import PartitionSpec as P

F32 = jnp.float32
BF16 = jnp.bfloat16
HIGHEST = lax.Precision.HIGHEST
VMEM = pltpu.VMEM
BLOCK = 128
GROUP = 8
TILE = 512
COST = pl.CostEstimate(flops=1, bytes_accessed=1, transcendentals=0)


def params(megabytes):
    return pltpu.CompilerParams(vmem_limit_bytes=megabytes * 1024 * 1024)


def whole(count):
    return [pl.BlockSpec(memory_space=VMEM)] * count


def dot(a, b, contract, precision=None):
    return lax.dot_general(
        a, b, ((contract[:1], contract[1:]), ((), ())), precision=precision, preferred_element_type=F32
    )


def split(x):
    high = x.astype(BF16)
    return high, (x - high.astype(F32)).astype(BF16)


def dot3(a, b, contract):
    ah, al = split(a)
    bh, bl = split(b)
    return dot(ah, bh, contract) + (dot(ah, bl, contract) + dot(al, bh, contract))


def pick_kernel(starts, side_ref, s_hbm, out_hbm, buffer, in_sems, out_sems):
    count, rows = buffer.shape[:2]
    start = pl.multiple_of(jnp.where(side_ref[0] == 0, starts[0], starts[1]), TILE)
    ins, outs = [], []
    for k in range(count):
        here = pl.ds(k * rows, rows)
        ins.append(pltpu.make_async_copy(s_hbm.at[pl.ds(start + k * rows, rows)], buffer.at[k], in_sems.at[k]))
        outs.append(pltpu.make_async_copy(buffer.at[k], out_hbm.at[here], out_sems.at[k]))
    for copy in ins:
        copy.start()
    for before, after in zip(ins, outs):
        before.wait()
        after.start()
    for copy in outs:
        copy.wait()


def pick(side, s, starts, rows):
    hbm = pl.BlockSpec(memory_space=pltpu.HBM)
    return pl.pallas_call(
        functools.partial(pick_kernel, starts),
        in_specs=[pl.BlockSpec(memory_space=pltpu.SMEM), hbm],
        out_specs=hbm,
        out_shape=jax.ShapeDtypeStruct((rows, s.shape[1]), F32),
        scratch_shapes=[
            pltpu.VMEM((4, rows // 4, s.shape[1]), F32),
            pltpu.SemaphoreType.DMA((4,)),
            pltpu.SemaphoreType.DMA((4,)),
        ],
        compiler_params=params(60),
        cost_estimate=COST,
        name="pick",
    )(side, s)


def block_pairs(blocks):
    return [(i, j) for i in range(blocks) for j in range(i, blocks)]


def own_gram_kernel(scale, spans, side_ref, s_ref, g_ref, *refs):
    copies, (high_acc, low_acc) = refs[:-2], refs[-2:]
    step = pl.program_id(0)
    order = low_acc.shape[0]

    @pl.when(step == 0)
    def _():
        high_acc[...] = jnp.zeros_like(high_acc)
        low_acc[...] = jnp.zeros_like(low_acc)

    block = s_ref[...]
    for copy, (start, shift, count) in zip(copies, spans):
        begin = start + shift * side_ref[0]

        @pl.when((step >= begin) & (step < begin + count))
        def _():
            copy[...] = block

    high, low = split(block)
    high_acc[...] += dot(high, jnp.concatenate([high, low], axis=1), (0, 0))
    low_acc[...] += dot(low, low, (0, 0))

    @pl.when(step == pl.num_programs(0) - 1)
    def _():
        for k, (i, j) in enumerate(block_pairs(order // BLOCK)):
            rows, columns = pl.ds(i * BLOCK, BLOCK), pl.ds(j * BLOCK, BLOCK)
            mixed = high_acc[rows, pl.ds(order + j * BLOCK, BLOCK)] + high_acc[columns, pl.ds(order + i * BLOCK, BLOCK)].T
            g_ref[pl.ds(k * BLOCK, BLOCK), :] = (high_acc[rows, columns] + (mixed + low_acc[rows, columns])) * scale


def own_gram(side, s, scale, spans):
    rows, width = s.shape
    square = (width, width)
    packed = (len(block_pairs(width // BLOCK)) * BLOCK, BLOCK)

    def copy_spec(start, shift, count):
        return pl.BlockSpec((TILE, width), lambda i, side: (jnp.clip(i - start - shift * side[0], 0, count - 1), 0))

    return pl.pallas_call(
        functools.partial(own_gram_kernel, scale, spans),
        grid_spec=pltpu.PrefetchScalarGridSpec(
            num_scalar_prefetch=1,
            grid=(rows // TILE,),
            in_specs=[pl.BlockSpec((TILE, width), lambda i, side: (i, 0))],
            out_specs=[pl.BlockSpec(packed, lambda i, side: (0, 0))] + [copy_spec(*span) for span in spans],
            scratch_shapes=[pltpu.VMEM((width, 2 * width), F32), pltpu.VMEM(square, F32)],
        ),
        out_shape=[jax.ShapeDtypeStruct(packed, F32)]
        + [jax.ShapeDtypeStruct((count * TILE, width), F32) for _, _, count in spans],
        compiler_params=params(60),
        cost_estimate=COST,
        name="own_gram",
    )(side, s)


def cross_gram_kernel(scale, resume, counts, side_ref, own_ref, *refs):
    chunks, before_ref, g_ref, acc = refs[: len(counts)], refs[len(counts)], refs[-2], refs[-1]
    step = pl.program_id(0)
    first = side_ref[0] == 0

    @pl.when(step == 0)
    def _():
        acc[...] = jnp.zeros_like(acc)

    begin = 0
    for chunk, count in zip(chunks, counts):

        @pl.when((step >= begin) & (step < begin + count))
        def _():
            own, other = own_ref[...], chunk[...]
            left = jnp.where(first, own, other)
            right = jnp.where(first, other, own)
            lh, ll = split(left)
            rh, rl = split(right * scale)
            right = jnp.concatenate([rh, rl], axis=1)
            acc[...] += dot(jnp.concatenate([lh, ll]), jnp.concatenate([right, right]), (0, 0))

        begin += count

    @pl.when(step == pl.num_programs(0) - 1)
    def _():
        width = g_ref.shape[0]
        total = acc[:, :width] + acc[:, width:]
        g_ref[...] = before_ref[...] + total if resume else total


def cross_gram(side, own, chunks, before, after, offset, scale):
    rows, width = own.shape
    counts = tuple(c.shape[0] // TILE for c in chunks)
    starts = [sum(counts[:i]) for i in range(len(counts))]
    square = (width, width)
    half = rows // 2 // TILE
    start = offset // TILE

    def chunk_spec(begin, count):
        return pl.BlockSpec((TILE, width), lambda i, side: (jnp.clip(i - begin, 0, count - 1), 0))

    in_specs = [pl.BlockSpec((TILE, width), lambda i, side: (i + start + (1 - side[0]) * half, 0))]
    in_specs += [chunk_spec(b, c) for b, c in zip(starts, counts)]
    in_specs += [pl.BlockSpec(square, lambda i, side: (0, 0))] * (before is not None)
    in_specs += [pl.BlockSpec(memory_space=pl.ANY)] * len(after)
    return pl.pallas_call(
        functools.partial(cross_gram_kernel, scale, before is not None, counts),
        grid_spec=pltpu.PrefetchScalarGridSpec(
            num_scalar_prefetch=1,
            grid=(sum(counts),),
            in_specs=in_specs,
            out_specs=pl.BlockSpec(square, lambda i, side: (0, 0)),
            scratch_shapes=[pltpu.VMEM((width, 2 * width), F32)],
        ),
        out_shape=jax.ShapeDtypeStruct(square, F32),
        compiler_params=params(60),
        cost_estimate=COST,
        name="cross_gram",
    )(side, own, *chunks, *([] if before is None else [before]), *after)


def factor_block(a, x):
    count, width = len(a), a[0].shape[1]
    shape = (GROUP, width)
    row = lax.broadcasted_iota(jnp.int32, shape, 0)
    lane = lax.broadcasted_iota(jnp.int32, shape, 1)
    upper, inverse = [], []
    for p in range(count):
        c = GROUP * p
        pa = [jnp.broadcast_to(a[p][k : k + 1, :], shape) for k in range(GROUP)]
        px = [jnp.broadcast_to(x[p][k : k + 1, :], shape) for k in range(GROUP)]
        s = [
            [jnp.broadcast_to(pa[k][:, c + l : c + l + 1], shape) if l >= k else None for l in range(GROUP)]
            for k in range(GROUP)
        ]
        reciprocal = []
        for k in range(GROUP):
            reciprocal.append(1.0 / s[k][k])
            for l in range(k + 1, GROUP):
                m = s[k][l] * reciprocal[k]
                for t in range(l, GROUP):
                    s[l][t] = s[l][t] - m * s[k][t]
                pa[l] = pa[l] - m * pa[k]
                px[l] = px[l] - m * px[k]
        for r in range(p + 1, count):
            columns = [jnp.broadcast_to(a[r][:, c + l : c + l + 1], shape) for l in range(GROUP)]
            for k in range(GROUP):
                m = columns[k] * reciprocal[k]
                for t in range(k + 1, GROUP):
                    columns[t] = columns[t] - m * s[k][t]
                a[r] = a[r] - m * pa[k]
                x[r] = x[r] - m * px[k]
        ua, ux = None, None
        for k in range(GROUP):
            root = lax.rsqrt(s[k][k])
            va, vx = pa[k] * root, px[k] * root
            ua = va if k == 0 else jnp.where(row == k, va, ua)
            ux = vx if k == 0 else jnp.where(row == k, vx, ux)
        upper.append(jnp.where(lane >= row + c, ua, 0.0))
        inverse.append(ux)
    return upper, inverse


def factor_whole(a_ref, r_ref, x_ref, e_ref, beside=None):
    order = a_ref.shape[0]
    blocks = order // BLOCK
    groups = BLOCK // GROUP
    r_ref[...] = jnp.zeros_like(r_ref)
    x_ref[...] = jnp.zeros_like(x_ref)
    row = lax.broadcasted_iota(jnp.int32, (GROUP, BLOCK), 0)
    lane = lax.broadcasted_iota(jnp.int32, (GROUP, BLOCK), 1)

    def body(b, carry):
        start = pl.multiple_of(b * BLOCK, BLOCK)
        here = pl.ds(start, BLOCK)
        a = [a_ref[pl.ds(start + GROUP * i, GROUP), here] for i in range(groups)]
        x = [jnp.where(lane == row + GROUP * i, 1.0, 0.0) for i in range(groups)]
        if beside is not None:
            beside(b, blocks)
        upper, inverse = factor_block(a, x)
        for i in range(groups):
            r_ref[pl.ds(start + GROUP * i, GROUP), here] = upper[i]
            e_ref[pl.ds(GROUP * i, GROUP), :] = inverse[i]
        for k in range(blocks):

            @pl.when(b == k)
            def _():
                lo, hi = k * BLOCK, (k + 1) * BLOCK
                e = e_ref[...]
                x_ref[lo:hi, lo:hi] = e
                if k > 0:
                    x_ref[lo:hi, :lo] = dot(e, x_ref[lo:hi, :lo], (1, 0), HIGHEST)
                if hi < order:
                    strip = dot(e, a_ref[lo:hi, hi:], (1, 0), HIGHEST)
                    r_ref[lo:hi, hi:] = strip
                    a_ref[hi:, hi:] -= dot(strip, strip, (0, 0), HIGHEST)
                    x_ref[hi:, :hi] -= dot(strip, x_ref[lo:hi, :hi], (0, 0), HIGHEST)

        return carry

    lax.fori_loop(0, blocks, body, 0)


def unpack(packed_ref, a_ref):
    for k, (i, j) in enumerate(block_pairs(a_ref.shape[0] // BLOCK)):
        a_ref[pl.ds(i * BLOCK, BLOCK), pl.ds(j * BLOCK, BLOCK)] = packed_ref[pl.ds(k * BLOCK, BLOCK), :]


def first_factor_kernel(start, g_ref, s_hbm, r_ref, x_ref, *refs):
    sends, (a_ref, e_ref, buffer, in_sem, out_sems) = refs[:-5], refs[-5:]
    load = pltpu.make_async_copy(s_hbm.at[pl.ds(start, buffer.shape[0])], buffer, in_sem)
    load.start()
    stores, begin = [], 0
    for k, send in enumerate(sends):
        here = pl.ds(begin, send.shape[0])
        stores.append(pltpu.make_async_copy(buffer.at[here], send, out_sems.at[k]))
        begin += send.shape[0]

    def beside(b, blocks):
        @pl.when(b == blocks - 2)
        def _():
            load.wait()
            for store in stores:
                store.start()

    unpack(g_ref, a_ref)
    factor_whole(a_ref, r_ref, x_ref, e_ref, beside)
    for store in stores:
        store.wait()


def first_factor(packed, order, own, start, sizes):
    square = jax.ShapeDtypeStruct((order, order), F32)
    hbm = pl.BlockSpec(memory_space=pltpu.HBM)
    return pl.pallas_call(
        functools.partial(first_factor_kernel, start),
        out_shape=[square, square] + [jax.ShapeDtypeStruct((size, order), F32) for size in sizes],
        in_specs=whole(1) + [hbm],
        out_specs=whole(2) + [hbm] * len(sizes),
        scratch_shapes=[
            pltpu.VMEM((order, order), F32),
            pltpu.VMEM((BLOCK, BLOCK), F32),
            pltpu.VMEM((sum(sizes), order), F32),
            pltpu.SemaphoreType.DMA,
            pltpu.SemaphoreType.DMA((len(sizes),)),
        ],
        compiler_params=params(60),
        cost_estimate=COST,
        name="first_factor",
    )(packed, own)


def thrice(x):
    high, low = split(x)
    return jnp.concatenate([high, high, low], axis=1)


def stacked(w):
    high, low = split(w)
    return jnp.concatenate([high, low, high], axis=0)


def times_upper(x, left, right):
    half = x.shape[1] // 2
    return jnp.concatenate(
        [dot(thrice(x[:, :half]), left, (1, 0)), dot(thrice(x), right, (1, 0))], axis=1
    )


def finish_kernel(counts, side_ref, cross_ref, g_ref, r00_ref, x0_ref, own_hbm, *refs):
    chunks, refs = refs[: len(counts)], refs[len(counts) :]
    f_hbm, share_hbm, part_hbm, basis_hbm = refs[:4]
    own, other, f_ref, share, u_ref, left_ref, right_ref, a_ref, r_ref, x_ref, e_ref = refs[4:15]
    load_sems, store_sems, out_sems = refs[15:]
    order = a_ref.shape[0]
    half = order // 2
    rows, known = own.shape[0], sum(counts)
    first = side_ref[0] == 0
    loads = [pltpu.make_async_copy(own_hbm, own, load_sems.at[len(counts)])]
    begin = 0
    for k, count in enumerate(counts):
        loads.append(pltpu.make_async_copy(chunks[k], other.at[pl.ds(begin, count)], load_sems.at[k]))
        begin += count
    for load in loads:
        load.start()
    outs = [
        pltpu.make_async_copy(f_ref.at[pl.ds(0, order)], f_hbm.at[pl.ds(0, order)], out_sems.at[0]),
        pltpu.make_async_copy(f_ref.at[pl.ds(order, order)], f_hbm.at[pl.ds(order, order)], out_sems.at[1]),
        pltpu.make_async_copy(share, share_hbm, out_sems.at[2]),
    ]
    x0 = x0_ref[...]
    r01 = dot(x0, cross_ref[...], (1, 0), HIGHEST)
    u = dot3(x0, r01, (0, 0))
    u_ref[...] = stacked(jnp.where(first, 0.0, u))
    unpack(g_ref, a_ref)
    a_ref[...] -= dot(r01, r01, (0, 0), HIGHEST)
    f_ref[:order] = jnp.where(first, r00_ref[...], r01)
    outs[0].start()
    for load in loads:
        load.wait()

    def project(b, blocks):
        size = other.shape[0] // blocks
        tile = math.gcd(size, TILE)
        for k in range(size // tile):
            here = pl.ds(pl.multiple_of(b * size + k * tile, tile), tile)
            own[here] -= dot(thrice(other[here]), u_ref[...], (1, 0))

    factor_whole(a_ref, r_ref, x_ref, e_ref, project)
    f_ref[order:] = jnp.where(first, 0.0, r_ref[...])
    outs[1].start()
    x1 = x_ref[...]
    share[...] = stacked(jnp.where(first, 0.0, -dot3(u, x1, (1, 1))))
    outs[2].start()
    w = jnp.where(first, x0, x1).T
    left_ref[...] = stacked(w[:half, :half])
    right_ref[...] = stacked(w[:, half:])

    def store(k):
        here = pl.ds(pl.multiple_of(k * TILE, TILE), TILE)
        return pltpu.make_async_copy(own.at[here], basis_hbm.at[here], store_sems.at[k])

    def body(k, carry):
        here = pl.ds(pl.multiple_of(k * TILE, TILE), TILE)
        own[here] = times_upper(own[here], left_ref[...], right_ref[...])
        store(k).start()
        return carry

    parts = []
    for k in range(known, rows, TILE):
        here = pl.ds(k, TILE)
        own[here] = times_upper(own[here], left_ref[...], right_ref[...])
        parts.append(pltpu.make_async_copy(own.at[here], part_hbm.at[pl.ds(k - known, TILE)], store_sems.at[k // TILE]))
        parts[-1].start()
    lax.fori_loop(0, known // TILE, body, 0)
    for part in parts:
        part.wait()
    for k in range(known // TILE):
        store(k).wait()
    for out in outs:
        out.wait()


def finish(side, cross, packed, r00, x0, own, chunks):
    order = cross.shape[0]
    half = order // 2
    square = (order, order)
    counts = tuple(c.shape[0] for c in chunks)
    anywhere = pl.BlockSpec(memory_space=pltpu.HBM)
    return pl.pallas_call(
        functools.partial(finish_kernel, counts),
        out_shape=[
            jax.ShapeDtypeStruct((2 * order, order), F32),
            jax.ShapeDtypeStruct((3 * order, order), BF16),
            jax.ShapeDtypeStruct((own.shape[0] - sum(counts), order), F32),
            jax.ShapeDtypeStruct(own.shape, F32),
        ],
        in_specs=[pl.BlockSpec(memory_space=pltpu.SMEM)] + whole(4) + [anywhere] * (1 + len(chunks)),
        out_specs=[anywhere] * 4,
        scratch_shapes=[
            pltpu.VMEM(own.shape, F32),
            pltpu.VMEM((sum(counts), order), F32),
            pltpu.VMEM((2 * order, order), F32),
            pltpu.VMEM((3 * order, order), BF16),
            pltpu.VMEM((3 * order, order), BF16),
            pltpu.VMEM((3 * half, half), BF16),
            pltpu.VMEM((3 * order, half), BF16),
            pltpu.VMEM(square, F32),
            pltpu.VMEM(square, F32),
            pltpu.VMEM(square, F32),
            pltpu.VMEM((BLOCK, BLOCK), F32),
            pltpu.SemaphoreType.DMA((len(chunks) + 1,)),
            pltpu.SemaphoreType.DMA((own.shape[0] // TILE,)),
            pltpu.SemaphoreType.DMA((3,)),
        ],
        compiler_params=params(60),
        cost_estimate=COST,
        name="finish",
    )(side, cross, packed, r00, x0, own, *chunks)


def stage_kernel(factor_ref, part_ref, factor_out, part_out):
    factor_out[...] = factor_ref[...]
    part_out[...] = part_ref[...]


def stage(factor, part):
    return pl.pallas_call(
        stage_kernel,
        in_specs=whole(2),
        out_specs=whole(2),
        out_shape=[jax.ShapeDtypeStruct(factor.shape, BF16), jax.ShapeDtypeStruct(part.shape, F32)],
        compiler_params=params(12),
        cost_estimate=COST,
        name="stage",
    )(factor, part)


def tail_kernel(start, row, chunk_ref, factor_ref, part_ref, before_hbm, basis_hbm, out, sems):
    copies = []
    for k in range(out.shape[0]):
        size = out.shape[1]
        here = pl.ds(k * size, size)
        out[k] = part_ref[pl.ds(start + k * size, size)] + dot(thrice(chunk_ref[here]), factor_ref[...], (1, 0))
        copies.append(pltpu.make_async_copy(out.at[k], basis_hbm.at[pl.ds(row + k * size, size)], sems.at[k]))
        copies[-1].start()
    for copy in copies:
        copy.wait()


def tail(chunk, factor, part, start, row, basis):
    rows, width = chunk.shape
    tile = math.gcd(TILE // 2, rows)
    anywhere = pl.BlockSpec(memory_space=pltpu.HBM)
    return pl.pallas_call(
        functools.partial(tail_kernel, start, row),
        in_specs=whole(3) + [anywhere],
        out_specs=anywhere,
        out_shape=jax.ShapeDtypeStruct(basis.shape, F32),
        scratch_shapes=[pltpu.VMEM((rows // tile, tile, width), F32), pltpu.SemaphoreType.DMA((rows // tile,))],
        input_output_aliases={3: 0},
        compiler_params=params(12),
        cost_estimate=COST,
        name="tail",
    )(chunk, factor, part, basis)


def flip(x, order, step):
    count = lax.axis_size("dof")
    return lax.ppermute(x, "dof", [(i, i ^ order[i % 2][step]) for i in range(count)])


def flip_side(x, order, sides):
    count = lax.axis_size("dof")
    pairs = [(2 * i + j, 2 * (i ^ order[i % 2][-1]) + 1 - j) for i in range(count) for j in sides]
    return lax.ppermute(x, ("dof", "snap"), pairs)


def halve(x, upper, send):
    half = x.shape[0] // 2
    low, high = x[:half], x[half:]
    return jnp.where(upper, high, low) + send(jnp.where(upper, low, high))


def double_with(x, other, upper, axis=0):
    return jnp.concatenate([jnp.where(upper, other, x), jnp.where(upper, x, other)], axis)


def double(x, upper, send, axis=0):
    return double_with(x, send(x), upper, axis)


def on_device(snapshots):
    rows, width = snapshots.shape
    count = lax.axis_size("dof")
    scale = 1.0 / (rows * count)
    me, side = lax.axis_index("dof"), lax.axis_index("snap")
    side_operand = jnp.full((1,), side, jnp.int32)
    bits = [1 << i for i in range(1, count.bit_length() - 1)]
    order = ([1] + bits[1:] + bits[:1], [1] + bits)
    steps = list(range(len(order[0])))

    def bit(step):
        return (me & jnp.where(me % 2 == 0, order[0][step], order[1][step])) != 0

    def send(step):
        return lambda x: flip(x, order, step)

    def reduce_own(i, carry):
        shard = carry[0]
        for k in steps:
            shard = halve(shard, bit(k), send(k))
        received = flip_side(shard, order, (0, 1))
        upper = bit(steps[-1]) ^ (side == 1)
        first = jnp.where(side == 0, shard, received)
        second = jnp.where(side == 0, received, shard)
        first = double(first, upper, send(steps[-1]))
        second = double(second, ~upper, send(steps[-1]))
        for k in steps[-2::-1]:
            first = double(first, bit(k), send(k))
            second = double(second, bit(k), send(k))
        return first, second

    def reduce_cross(i, cross):
        for k in steps[:-1]:
            cross = halve(cross, bit(k), send(k))
        cross = cross + flip_side(cross, order, (0,))
        cross = cross + send(steps[-1])(cross)
        for k in steps[-2::-1]:
            cross = double(cross, bit(k), send(k))
        return cross

    half = rows // 2 // TILE
    parts = [half // 4, half // 2, half - half // 4 - half // 2]
    spans = [(parts[0], half, parts[1]), (parts[0] + parts[1], half, parts[2])]
    middle = rows // 2
    rests = [middle // 2, middle // 2]

    def swap(x):
        return lax.ppermute(x, "snap", [(0, 1), (1, 0)])

    def one_way(x):
        return lax.ppermute(x, "snap", [(0, 1)])

    def late(x, after):
        return lax.optimization_barrier((x, after))[0]

    once = 1 + jnp.minimum(side, 0)
    arrived = [swap(pick(side_operand, snapshots, (0, half * TILE), parts[0] * TILE))]
    own, *sends = own_gram(side_operand, snapshots, scale, spans)
    arrived.append(swap(sends[0]))
    first, second = lax.fori_loop(0, once, reduce_own, (own, own))
    arrived.append(swap(late(sends[1], first)))
    r00, x00, *rest = first_factor(first, width, snapshots, middle, rests)
    arrived.append(one_way(rest[0]))
    early = parts[0] + parts[1]
    cross = cross_gram(side_operand, snapshots, arrived[:2], None, [x00, second], 0, scale)
    arrived.append(one_way(late(rest[1], cross)))
    cross = cross_gram(side_operand, snapshots, arrived[2:3], cross, [], early * TILE, scale)
    cross = lax.fori_loop(0, once, reduce_cross, cross)
    factor, share, part, basis = finish(side_operand, cross, second, r00, x00, snapshots, arrived[:4])
    share, part = stage(share, part)
    basis = tail(arrived[4], share, part, 0, middle + rests[0], basis)
    return (basis, factor)


def solution(mesh):
    in_specs = (P("dof", "snap"),)
    out_specs = (P("dof", "snap"), P(None, "snap"))
    return jax.shard_map(
        on_device, mesh=mesh, in_specs=in_specs, out_specs=out_specs, check_vma=False
    )
```

```python
import functools
import math

import jax
import jax.numpy as jnp
from jax import lax
from jax.experimental import pallas as pl
from jax.experimental.pallas import tpu as pltpu
from jax.sharding import PartitionSpec as P

F32 = jnp.float32
BF16 = jnp.bfloat16
HIGHEST = lax.Precision.HIGHEST
VMEM = pltpu.VMEM
BLOCK = 128
GROUP = 8
TILE = 512
COST = pl.CostEstimate(flops=1, bytes_accessed=1, transcendentals=0)


def params(megabytes):
    return pltpu.CompilerParams(vmem_limit_bytes=megabytes * 1024 * 1024)


def whole(count):
    return [pl.BlockSpec(memory_space=VMEM)] * count


def dot(a, b, contract, precision=None):
    return lax.dot_general(
        a, b, ((contract[:1], contract[1:]), ((), ())), precision=precision, preferred_element_type=F32
    )


def split(x):
    high = x.astype(BF16)
    return high, (x - high.astype(F32)).astype(BF16)


def dot3(a, b, contract):
    ah, al = split(a)
    bh, bl = split(b)
    return dot(ah, bh, contract) + (dot(ah, bl, contract) + dot(al, bh, contract))


def pick_kernel(starts, side_ref, s_hbm, out_hbm, buffer, in_sems, out_sems):
    count, rows = buffer.shape[:2]
    start = pl.multiple_of(jnp.where(side_ref[0] == 0, starts[0], starts[1]), TILE)
    ins, outs = [], []
    for k in range(count):
        here = pl.ds(k * rows, rows)
        ins.append(pltpu.make_async_copy(s_hbm.at[pl.ds(start + k * rows, rows)], buffer.at[k], in_sems.at[k]))
        outs.append(pltpu.make_async_copy(buffer.at[k], out_hbm.at[here], out_sems.at[k]))
    for copy in ins:
        copy.start()
    for before, after in zip(ins, outs):
        before.wait()
        after.start()
    for copy in outs:
        copy.wait()


def pick(side, s, starts, rows):
    hbm = pl.BlockSpec(memory_space=pltpu.HBM)
    return pl.pallas_call(
        functools.partial(pick_kernel, starts),
        in_specs=[pl.BlockSpec(memory_space=pltpu.SMEM), hbm],
        out_specs=hbm,
        out_shape=jax.ShapeDtypeStruct((rows, s.shape[1]), F32),
        scratch_shapes=[
            pltpu.VMEM((4, rows // 4, s.shape[1]), F32),
            pltpu.SemaphoreType.DMA((4,)),
            pltpu.SemaphoreType.DMA((4,)),
        ],
        compiler_params=params(60),
        cost_estimate=COST,
        name="pick",
    )(side, s)


def block_pairs(blocks):
    return [(i, j) for i in range(blocks) for j in range(i, blocks)]


def own_gram_kernel(scale, spans, side_ref, s_ref, g_ref, *refs):
    copies, (high_acc, low_acc) = refs[:-2], refs[-2:]
    step = pl.program_id(0)
    order = low_acc.shape[0]

    @pl.when(step == 0)
    def _():
        high_acc[...] = jnp.zeros_like(high_acc)
        low_acc[...] = jnp.zeros_like(low_acc)

    block = s_ref[...]
    for copy, (start, shift, count) in zip(copies, spans):
        begin = start + shift * side_ref[0]

        @pl.when((step >= begin) & (step < begin + count))
        def _():
            copy[...] = block

    high, low = split(block)
    high_acc[...] += dot(high, jnp.concatenate([high, low], axis=1), (0, 0))
    low_acc[...] += dot(low, low, (0, 0))

    @pl.when(step == pl.num_programs(0) - 1)
    def _():
        for k, (i, j) in enumerate(block_pairs(order // BLOCK)):
            rows, columns = pl.ds(i * BLOCK, BLOCK), pl.ds(j * BLOCK, BLOCK)
            mixed = high_acc[rows, pl.ds(order + j * BLOCK, BLOCK)] + high_acc[columns, pl.ds(order + i * BLOCK, BLOCK)].T
            g_ref[pl.ds(k * BLOCK, BLOCK), :] = (high_acc[rows, columns] + (mixed + low_acc[rows, columns])) * scale


def own_gram(side, s, scale, spans):
    rows, width = s.shape
    square = (width, width)
    packed = (len(block_pairs(width // BLOCK)) * BLOCK, BLOCK)

    def copy_spec(start, shift, count):
        return pl.BlockSpec((TILE, width), lambda i, side: (jnp.clip(i - start - shift * side[0], 0, count - 1), 0))

    return pl.pallas_call(
        functools.partial(own_gram_kernel, scale, spans),
        grid_spec=pltpu.PrefetchScalarGridSpec(
            num_scalar_prefetch=1,
            grid=(rows // TILE,),
            in_specs=[pl.BlockSpec((TILE, width), lambda i, side: (i, 0))],
            out_specs=[pl.BlockSpec(packed, lambda i, side: (0, 0))] + [copy_spec(*span) for span in spans],
            scratch_shapes=[pltpu.VMEM((width, 2 * width), F32), pltpu.VMEM(square, F32)],
        ),
        out_shape=[jax.ShapeDtypeStruct(packed, F32)]
        + [jax.ShapeDtypeStruct((count * TILE, width), F32) for _, _, count in spans],
        compiler_params=params(60),
        cost_estimate=COST,
        name="own_gram",
    )(side, s)


def cross_gram_kernel(scale, resume, counts, side_ref, own_ref, *refs):
    chunks, before_ref, g_ref, acc = refs[: len(counts)], refs[len(counts)], refs[-2], refs[-1]
    step = pl.program_id(0)
    first = side_ref[0] == 0

    @pl.when(step == 0)
    def _():
        acc[...] = jnp.zeros_like(acc)

    begin = 0
    for chunk, count in zip(chunks, counts):

        @pl.when((step >= begin) & (step < begin + count))
        def _():
            own, other = own_ref[...], chunk[...]
            left = jnp.where(first, own, other)
            right = jnp.where(first, other, own)
            lh, ll = split(left)
            rh, rl = split(right * scale)
            right = jnp.concatenate([rh, rl], axis=1)
            acc[...] += dot(jnp.concatenate([lh, ll]), jnp.concatenate([right, right]), (0, 0))

        begin += count

    @pl.when(step == pl.num_programs(0) - 1)
    def _():
        width = g_ref.shape[0]
        total = acc[:, :width] + acc[:, width:]
        g_ref[...] = before_ref[...] + total if resume else total


def cross_gram(side, own, chunks, before, after, offset, scale):
    rows, width = own.shape
    counts = tuple(c.shape[0] // TILE for c in chunks)
    starts = [sum(counts[:i]) for i in range(len(counts))]
    square = (width, width)
    half = rows // 2 // TILE
    start = offset // TILE

    def chunk_spec(begin, count):
        return pl.BlockSpec((TILE, width), lambda i, side: (jnp.clip(i - begin, 0, count - 1), 0))

    in_specs = [pl.BlockSpec((TILE, width), lambda i, side: (i + start + (1 - side[0]) * half, 0))]
    in_specs += [chunk_spec(b, c) for b, c in zip(starts, counts)]
    in_specs += [pl.BlockSpec(square, lambda i, side: (0, 0))] * (before is not None)
    in_specs += [pl.BlockSpec(memory_space=pl.ANY)] * len(after)
    return pl.pallas_call(
        functools.partial(cross_gram_kernel, scale, before is not None, counts),
        grid_spec=pltpu.PrefetchScalarGridSpec(
            num_scalar_prefetch=1,
            grid=(sum(counts),),
            in_specs=in_specs,
            out_specs=pl.BlockSpec(square, lambda i, side: (0, 0)),
            scratch_shapes=[pltpu.VMEM((width, 2 * width), F32)],
        ),
        out_shape=jax.ShapeDtypeStruct(square, F32),
        compiler_params=params(60),
        cost_estimate=COST,
        name="cross_gram",
    )(side, own, *chunks, *([] if before is None else [before]), *after)


def factor_block(a, x):
    count, width = len(a), a[0].shape[1]
    shape = (GROUP, width)
    row = lax.broadcasted_iota(jnp.int32, shape, 0)
    lane = lax.broadcasted_iota(jnp.int32, shape, 1)
    upper, inverse = [], []
    for p in range(count):
        c = GROUP * p
        pa = [jnp.broadcast_to(a[p][k : k + 1, :], shape) for k in range(GROUP)]
        px = [jnp.broadcast_to(x[p][k : k + 1, :], shape) for k in range(GROUP)]
        corner = [jnp.broadcast_to(a[p][:, c + l : c + l + 1], shape) for l in range(GROUP)]
        s = [[jnp.broadcast_to(corner[l][k : k + 1, :], shape) for l in range(GROUP)] for k in range(GROUP)]
        reciprocal = []
        for k in range(GROUP):
            reciprocal.append(1.0 / s[k][k])
            for l in range(k + 1, GROUP):
                m = s[l][k] * reciprocal[k]
                for t in range(k + 1, GROUP):
                    s[l][t] = s[l][t] - m * s[k][t]
                pa[l] = pa[l] - m * pa[k]
                px[l] = px[l] - m * px[k]
        for r in range(p + 1, count):
            columns = [jnp.broadcast_to(a[r][:, c + l : c + l + 1], shape) for l in range(GROUP)]
            for k in range(GROUP):
                m = columns[k] * reciprocal[k]
                for t in range(k + 1, GROUP):
                    columns[t] = columns[t] - m * s[k][t]
                a[r] = a[r] - m * pa[k]
                x[r] = x[r] - m * px[k]
        ua, ux = None, None
        for k in range(GROUP):
            root = lax.rsqrt(s[k][k])
            va, vx = pa[k] * root, px[k] * root
            ua = va if k == 0 else jnp.where(row == k, va, ua)
            ux = vx if k == 0 else jnp.where(row == k, vx, ux)
        upper.append(jnp.where(lane >= row + c, ua, 0.0))
        inverse.append(ux)
    return upper, inverse


def factor_whole(a_ref, r_ref, x_ref, e_ref, beside=None):
    order = a_ref.shape[0]
    blocks = order // BLOCK
    groups = BLOCK // GROUP
    r_ref[...] = jnp.zeros_like(r_ref)
    x_ref[...] = jnp.zeros_like(x_ref)
    row = lax.broadcasted_iota(jnp.int32, (GROUP, BLOCK), 0)
    lane = lax.broadcasted_iota(jnp.int32, (GROUP, BLOCK), 1)

    def body(b, carry):
        start = pl.multiple_of(b * BLOCK, BLOCK)
        here = pl.ds(start, BLOCK)
        a = [a_ref[pl.ds(start + GROUP * i, GROUP), here] for i in range(groups)]
        x = [jnp.where(lane == row + GROUP * i, 1.0, 0.0) for i in range(groups)]
        if beside is not None:
            beside(b, blocks)
        upper, inverse = factor_block(a, x)
        for i in range(groups):
            r_ref[pl.ds(start + GROUP * i, GROUP), here] = upper[i]
            e_ref[pl.ds(GROUP * i, GROUP), :] = inverse[i]
        for k in range(blocks):

            @pl.when(b == k)
            def _():
                lo, hi = k * BLOCK, (k + 1) * BLOCK
                e = e_ref[...]
                x_ref[lo:hi, lo:hi] = e
                if k > 0:
                    x_ref[lo:hi, :lo] = dot(e, x_ref[lo:hi, :lo], (1, 0), HIGHEST)
                if hi < order:
                    strip = dot(e, a_ref[lo:hi, hi:], (1, 0), HIGHEST)
                    r_ref[lo:hi, hi:] = strip
                    a_ref[hi:, hi:] -= dot(strip, strip, (0, 0), HIGHEST)
                    x_ref[hi:, :hi] -= dot(strip, x_ref[lo:hi, :hi], (0, 0), HIGHEST)

        return carry

    lax.fori_loop(0, blocks, body, 0)


def unpack(packed_ref, a_ref):
    for k, (i, j) in enumerate(block_pairs(a_ref.shape[0] // BLOCK)):
        a_ref[pl.ds(i * BLOCK, BLOCK), pl.ds(j * BLOCK, BLOCK)] = packed_ref[pl.ds(k * BLOCK, BLOCK), :]


def first_factor_kernel(start, g_ref, s_hbm, r_ref, x_ref, *refs):
    sends, (a_ref, e_ref, buffer, in_sem, out_sems) = refs[:-5], refs[-5:]
    load = pltpu.make_async_copy(s_hbm.at[pl.ds(start, buffer.shape[0])], buffer, in_sem)
    load.start()
    stores, begin = [], 0
    for k, send in enumerate(sends):
        here = pl.ds(begin, send.shape[0])
        stores.append(pltpu.make_async_copy(buffer.at[here], send, out_sems.at[k]))
        begin += send.shape[0]

    def beside(b, blocks):
        @pl.when(b == blocks - 2)
        def _():
            load.wait()
            for store in stores:
                store.start()

    unpack(g_ref, a_ref)
    factor_whole(a_ref, r_ref, x_ref, e_ref, beside)
    for store in stores:
        store.wait()


def first_factor(packed, order, own, start, sizes):
    square = jax.ShapeDtypeStruct((order, order), F32)
    hbm = pl.BlockSpec(memory_space=pltpu.HBM)
    return pl.pallas_call(
        functools.partial(first_factor_kernel, start),
        out_shape=[square, square] + [jax.ShapeDtypeStruct((size, order), F32) for size in sizes],
        in_specs=whole(1) + [hbm],
        out_specs=whole(2) + [hbm] * len(sizes),
        scratch_shapes=[
            pltpu.VMEM((order, order), F32),
            pltpu.VMEM((BLOCK, BLOCK), F32),
            pltpu.VMEM((sum(sizes), order), F32),
            pltpu.SemaphoreType.DMA,
            pltpu.SemaphoreType.DMA((len(sizes),)),
        ],
        compiler_params=params(60),
        cost_estimate=COST,
        name="first_factor",
    )(packed, own)


def thrice(x):
    high, low = split(x)
    return jnp.concatenate([high, high, low], axis=1)


def stacked(w):
    high, low = split(w)
    return jnp.concatenate([high, low, high], axis=0)


def times_upper(x, left, right):
    half = x.shape[1] // 2
    return jnp.concatenate(
        [dot(thrice(x[:, :half]), left, (1, 0)), dot(thrice(x), right, (1, 0))], axis=1
    )


def finish_kernel(counts, side_ref, cross_ref, g_ref, r00_ref, x0_ref, own_hbm, *refs):
    chunks, refs = refs[: len(counts)], refs[len(counts) :]
    f_hbm, share_hbm, part_hbm, basis_hbm = refs[:4]
    own, other, f_ref, share, u_ref, left_ref, right_ref, a_ref, r_ref, x_ref, e_ref = refs[4:15]
    load_sems, store_sems, out_sems = refs[15:]
    order = a_ref.shape[0]
    half = order // 2
    rows, known = own.shape[0], sum(counts)
    first = side_ref[0] == 0
    loads = [pltpu.make_async_copy(own_hbm, own, load_sems.at[len(counts)])]
    begin = 0
    for k, count in enumerate(counts):
        loads.append(pltpu.make_async_copy(chunks[k], other.at[pl.ds(begin, count)], load_sems.at[k]))
        begin += count
    for load in loads:
        load.start()
    outs = [
        pltpu.make_async_copy(f_ref.at[pl.ds(0, order)], f_hbm.at[pl.ds(0, order)], out_sems.at[0]),
        pltpu.make_async_copy(f_ref.at[pl.ds(order, order)], f_hbm.at[pl.ds(order, order)], out_sems.at[1]),
        pltpu.make_async_copy(share, share_hbm, out_sems.at[2]),
    ]
    x0 = x0_ref[...]
    r01 = dot(x0, cross_ref[...], (1, 0), HIGHEST)
    u = dot3(x0, r01, (0, 0))
    u_ref[...] = stacked(jnp.where(first, 0.0, u))
    unpack(g_ref, a_ref)
    a_ref[...] -= dot(r01, r01, (0, 0), HIGHEST)
    f_ref[:order] = jnp.where(first, r00_ref[...], r01)
    outs[0].start()
    for load in loads:
        load.wait()

    def project(b, blocks):
        size = other.shape[0] // blocks
        tile = math.gcd(size, TILE)
        for k in range(size // tile):
            here = pl.ds(pl.multiple_of(b * size + k * tile, tile), tile)
            own[here] -= dot(thrice(other[here]), u_ref[...], (1, 0))

    factor_whole(a_ref, r_ref, x_ref, e_ref, project)
    f_ref[order:] = jnp.where(first, 0.0, r_ref[...])
    outs[1].start()
    x1 = x_ref[...]
    share[...] = stacked(jnp.where(first, 0.0, -dot3(u, x1, (1, 1))))
    outs[2].start()
    w = jnp.where(first, x0, x1).T
    left_ref[...] = stacked(w[:half, :half])
    right_ref[...] = stacked(w[:, half:])

    def store(k):
        here = pl.ds(pl.multiple_of(k * TILE, TILE), TILE)
        return pltpu.make_async_copy(own.at[here], basis_hbm.at[here], store_sems.at[k])

    def body(k, carry):
        here = pl.ds(pl.multiple_of(k * TILE, TILE), TILE)
        own[here] = times_upper(own[here], left_ref[...], right_ref[...])
        store(k).start()
        return carry

    parts = []
    for k in range(known, rows, TILE):
        here = pl.ds(k, TILE)
        own[here] = times_upper(own[here], left_ref[...], right_ref[...])
        parts.append(pltpu.make_async_copy(own.at[here], part_hbm.at[pl.ds(k - known, TILE)], store_sems.at[k // TILE]))
        parts[-1].start()
    lax.fori_loop(0, known // TILE, body, 0)
    for part in parts:
        part.wait()
    for k in range(known // TILE):
        store(k).wait()
    for out in outs:
        out.wait()


def finish(side, cross, packed, r00, x0, own, chunks):
    order = cross.shape[0]
    half = order // 2
    square = (order, order)
    counts = tuple(c.shape[0] for c in chunks)
    anywhere = pl.BlockSpec(memory_space=pltpu.HBM)
    return pl.pallas_call(
        functools.partial(finish_kernel, counts),
        out_shape=[
            jax.ShapeDtypeStruct((2 * order, order), F32),
            jax.ShapeDtypeStruct((3 * order, order), BF16),
            jax.ShapeDtypeStruct((own.shape[0] - sum(counts), order), F32),
            jax.ShapeDtypeStruct(own.shape, F32),
        ],
        in_specs=[pl.BlockSpec(memory_space=pltpu.SMEM)] + whole(4) + [anywhere] * (1 + len(chunks)),
        out_specs=[anywhere] * 4,
        scratch_shapes=[
            pltpu.VMEM(own.shape, F32),
            pltpu.VMEM((sum(counts), order), F32),
            pltpu.VMEM((2 * order, order), F32),
            pltpu.VMEM((3 * order, order), BF16),
            pltpu.VMEM((3 * order, order), BF16),
            pltpu.VMEM((3 * half, half), BF16),
            pltpu.VMEM((3 * order, half), BF16),
            pltpu.VMEM(square, F32),
            pltpu.VMEM(square, F32),
            pltpu.VMEM(square, F32),
            pltpu.VMEM((BLOCK, BLOCK), F32),
            pltpu.SemaphoreType.DMA((len(chunks) + 1,)),
            pltpu.SemaphoreType.DMA((own.shape[0] // TILE,)),
            pltpu.SemaphoreType.DMA((3,)),
        ],
        compiler_params=params(60),
        cost_estimate=COST,
        name="finish",
    )(side, cross, packed, r00, x0, own, *chunks)


def stage_kernel(factor_ref, part_ref, factor_out, part_out):
    factor_out[...] = factor_ref[...]
    part_out[...] = part_ref[...]


def stage(factor, part):
    return pl.pallas_call(
        stage_kernel,
        in_specs=whole(2),
        out_specs=whole(2),
        out_shape=[jax.ShapeDtypeStruct(factor.shape, BF16), jax.ShapeDtypeStruct(part.shape, F32)],
        compiler_params=params(12),
        cost_estimate=COST,
        name="stage",
    )(factor, part)


def tail_kernel(start, row, chunk_ref, factor_ref, part_ref, before_hbm, basis_hbm, out, sems):
    copies = []
    for k in range(out.shape[0]):
        size = out.shape[1]
        here = pl.ds(k * size, size)
        out[k] = part_ref[pl.ds(start + k * size, size)] + dot(thrice(chunk_ref[here]), factor_ref[...], (1, 0))
        copies.append(pltpu.make_async_copy(out.at[k], basis_hbm.at[pl.ds(row + k * size, size)], sems.at[k]))
        copies[-1].start()
    for copy in copies:
        copy.wait()


def tail(chunk, factor, part, start, row, basis):
    rows, width = chunk.shape
    tile = math.gcd(TILE // 2, rows)
    anywhere = pl.BlockSpec(memory_space=pltpu.HBM)
    return pl.pallas_call(
        functools.partial(tail_kernel, start, row),
        in_specs=whole(3) + [anywhere],
        out_specs=anywhere,
        out_shape=jax.ShapeDtypeStruct(basis.shape, F32),
        scratch_shapes=[pltpu.VMEM((rows // tile, tile, width), F32), pltpu.SemaphoreType.DMA((rows // tile,))],
        input_output_aliases={3: 0},
        compiler_params=params(12),
        cost_estimate=COST,
        name="tail",
    )(chunk, factor, part, basis)


def flip(x, order, step):
    count = lax.axis_size("dof")
    return lax.ppermute(x, "dof", [(i, i ^ order[i % 2][step]) for i in range(count)])


def flip_side(x, order, sides):
    count = lax.axis_size("dof")
    pairs = [(2 * i + j, 2 * (i ^ order[i % 2][-1]) + 1 - j) for i in range(count) for j in sides]
    return lax.ppermute(x, ("dof", "snap"), pairs)


def halve(x, upper, send):
    half = x.shape[0] // 2
    low, high = x[:half], x[half:]
    return jnp.where(upper, high, low) + send(jnp.where(upper, low, high))


def double_with(x, other, upper, axis=0):
    return jnp.concatenate([jnp.where(upper, other, x), jnp.where(upper, x, other)], axis)


def double(x, upper, send, axis=0):
    return double_with(x, send(x), upper, axis)


def on_device(snapshots):
    rows, width = snapshots.shape
    count = lax.axis_size("dof")
    scale = 1.0 / (rows * count)
    me, side = lax.axis_index("dof"), lax.axis_index("snap")
    side_operand = jnp.full((1,), side, jnp.int32)
    bits = [1 << i for i in range(1, count.bit_length() - 1)]
    order = ([1] + bits[1:] + bits[:1], [1] + bits)
    steps = list(range(len(order[0])))

    def bit(step):
        return (me & jnp.where(me % 2 == 0, order[0][step], order[1][step])) != 0

    def send(step):
        return lambda x: flip(x, order, step)

    def reduce_own(i, carry):
        shard = carry[0]
        for k in steps:
            shard = halve(shard, bit(k), send(k))
        received = flip_side(shard, order, (0, 1))
        upper = bit(steps[-1]) ^ (side == 1)
        first = jnp.where(side == 0, shard, received)
        second = jnp.where(side == 0, received, shard)
        first = double(first, upper, send(steps[-1]))
        second = double(second, ~upper, send(steps[-1]))
        for k in steps[-2::-1]:
            first = double(first, bit(k), send(k))
            second = double(second, bit(k), send(k))
        return first, second

    def reduce_cross(i, cross):
        for k in steps[:-1]:
            cross = halve(cross, bit(k), send(k))
        cross = cross + flip_side(cross, order, (0,))
        cross = cross + send(steps[-1])(cross)
        for k in steps[-2::-1]:
            cross = double(cross, bit(k), send(k))
        return cross

    half = rows // 2 // TILE
    parts = [half // 4, half // 2, half - half // 4 - half // 2]
    spans = [(parts[0], half, parts[1]), (parts[0] + parts[1], half, parts[2])]
    middle = rows // 2
    rests = [middle // 2, middle // 2]

    def swap(x):
        return lax.ppermute(x, "snap", [(0, 1), (1, 0)])

    def one_way(x):
        return lax.ppermute(x, "snap", [(0, 1)])

    def late(x, after):
        return lax.optimization_barrier((x, after))[0]

    once = 1 + jnp.minimum(side, 0)
    arrived = [swap(pick(side_operand, snapshots, (0, half * TILE), parts[0] * TILE))]
    own, *sends = own_gram(side_operand, snapshots, scale, spans)
    arrived.append(swap(sends[0]))
    first, second = lax.fori_loop(0, once, reduce_own, (own, own))
    arrived.append(swap(late(sends[1], first)))
    r00, x00, *rest = first_factor(first, width, snapshots, middle, rests)
    arrived.append(one_way(rest[0]))
    early = parts[0] + parts[1]
    cross = cross_gram(side_operand, snapshots, arrived[:2], None, [x00, second], 0, scale)
    arrived.append(one_way(late(rest[1], cross)))
    cross = cross_gram(side_operand, snapshots, arrived[2:3], cross, [], early * TILE, scale)
    cross = lax.fori_loop(0, once, reduce_cross, cross)
    factor, share, part, basis = finish(side_operand, cross, second, r00, x00, snapshots, arrived[:4])
    share, part = stage(share, part)
    basis = tail(arrived[4], share, part, 0, middle + rests[0], basis)
    return (basis, factor)


def solution(mesh):
    in_specs = (P("dof", "snap"),)
    out_specs = (P("dof", "snap"), P(None, "snap"))
    return jax.shard_map(
        on_device, mesh=mesh, in_specs=in_specs, out_specs=out_specs, check_vma=False
    )
```
